32 devices in a mesh: rep: 2 (over x), attn: 16 (over z, y, core).
Axes of the slice: x: 2, y: 2, z: 4, core: 2. Of those that a mesh axis runs over, the one named last changes fastest.
Arguments:
- moe_input: bfloat16 [768, 7168], P(('rep', 'attn')), parts along dimension 0, may hold values from -6 to 6
- expert_ids: int32 [768, 2], P(('rep', 'attn')), parts along dimension 0, may hold values from 0 to 7, all different within a row; in each aligned block of 24 rows (0 to 23, 24 to 47, ...) at most 9 rows name the same one
- route_scores: float32 [768, 2], P(('rep', 'attn')), parts along dimension 0, may hold values from 0.05 to 1
- gate_weight: bfloat16 [7168, 8192], P(None, 'attn'), may hold values from -0.0625 to 0.0625
- up_weight: bfloat16 [7168, 8192], P(None, 'attn'), may hold values from -0.0625 to 0.0625
- down_weight: bfloat16 [8192, 7168], P('attn'), may hold values from -0.1875 to 0.1875
- q_latent: bfloat16 [192, 4, 32768], P(('rep', 'attn')), parts along dimension 0, may hold values from -6 to 6
- q_rope: bfloat16 [192, 4, 4096], P(('rep', 'attn')), parts along dimension 0, may hold values from -450 to 450
- latent_cache: bfloat16 [192, 256, 512], P(('rep', 'attn')), parts along dimension 0, may hold values from -6 to 6
- rope_cache: bfloat16 [192, 256, 64], P(('rep', 'attn')), parts along dimension 0, may hold values from -6 to 6
- cache_lengths: int32 [192], P(('rep', 'attn')), parts along dimension 0, may hold values from 6 to 256, as said below
Outputs:
- moe_output: bfloat16 [768, 7168], P(('rep', 'attn')), parts along dimension 0
- attn_output: bfloat16 [192, 4, 32768], P(('rep', 'attn')), parts along dimension 0
The draws below stay inside these ranges and needn't reach their ends.
There are 2 independent parts, one for each index of `rep`. The reference program is written for one: setup_inputs(seed, part) draws one part's arguments, and reference() takes and returns one part's arrays. A program takes and returns all parts, laid end to end along the dimension named above; an argument that names none is the same for every part. Nothing has to cross between parts.
Inputs may be any that keep to these rules, and one draw needn't show every extreme that they name: `expert_ids`: each row names 2 different experts. In each aligned block of 24 rows no expert is named by more than 9 rows, and in some block an expert is named by exactly 9 rows. `cache_lengths`: some sequence fills all 256 positions.
All inputs are finite; a program needn't handle non-finite values.
Results may differ from the reference program's by a relative error of at most 0.012.
Values may be sent and summed in bfloat16 or wider, within the bound.
No kernel may reach another device: no remote copies, remote signals or barrier semaphores. Data moves between devices by JAX's collectives and lax.ppermute only.
A program may use at most 128 MiB of HBM per device.

```python
import math
import jax
import jax.numpy as jnp
import numpy as np
from jax import lax

D = 7168
LATENT = 512
ROPE = 64
HEADS = 64
FFW = 1024
EXPERTS = 8
TOP = 2
STEPS = 4
LMAX = 256
ROWS = 24
CAP = 9
SHARDS = 2
FF_DEV = 512
TOKENS = 384
SEQS = 96
N_ATTN = 16


def rope_pattern(key):
    return jnp.clip(jax.random.normal(key, (SEQS, LMAX, ROPE), jnp.float32), -6.0, 6.0)


def draw_rope_cache(key, part):
    values = rope_pattern(key)
    return values.astype(jnp.bfloat16)


def draw_q_rope(key, part):
    key = jax.random.fold_in(key, 11)
    values = jnp.clip(jax.random.normal(key, (SEQS, STEPS, HEADS, ROPE), jnp.float32), -6.0, 6.0)
    return values.reshape(SEQS, STEPS, HEADS * ROPE).astype(jnp.bfloat16)


def draw_cache_lengths(key, part):
    key = jax.random.fold_in(key, 5)
    first_key, second_key = jax.random.split(key)
    lengths = jax.random.randint(first_key, (SEQS,), STEPS + 2, LMAX + 1, jnp.int32)
    spot = jax.random.randint(second_key, (), 0, SEQS, jnp.int32)
    return lengths.at[spot].set(LMAX).astype(jnp.int32)


def shard_levels(key, shape, cuts, low, top_value):
    factor_of, own = 1.0, jax.random.fold_in(key, 6)
    for dim, parts in cuts:
        draws = jnp.exp(jax.random.uniform(jax.random.fold_in(own, dim), (parts,), jnp.float32, low / len(cuts), top_value / len(cuts)))
        factor_of = factor_of * jnp.repeat(draws, shape[dim] // parts).reshape([-1 if axis == dim else 1 for axis in range(len(shape))])
    return factor_of


def shared_out(rng, own, number, rows, count, top, most, slope):
    sequence = jax.random.permutation(rng, count)
    heavy_load, common = portions_of(count, rows * top, most, slope, True), portions_of(count, rows * top, most, slope, False)
    places = jnp.arange(count)

    def named(tallies, offset_by):
        used = int((tallies > 0).sum())
        fixed = max(1, used // 4)
        passed = fixed + (places - fixed + offset_by * (used - fixed)) % max(1, count - fixed)
        return jnp.zeros((count,), jnp.int32).at[sequence[jnp.where(places < fixed, places, passed)]].set(jnp.asarray(tallies, jnp.int32))

    tallies = jnp.where(number % 4 == 0, named(heavy_load, number // 4), named(common, number - number // 4 - 1))
    mixed = jax.random.permutation(jax.random.fold_in(own, 3), count)
    donor, receiver = mixed[0:count // 2 * 2:2], mixed[1:count // 2 * 2:2]
    slack = jnp.minimum(tallies[donor] - 1, most - tallies[receiver]) // 2
    slack = jnp.where((donor == sequence[0]) | (receiver == sequence[0]) | (tallies[receiver] == 0), 0, jnp.maximum(slack, 0))
    passed = jax.random.randint(jax.random.fold_in(own, 4), (count // 2,), 0, 1 << 20) % (slack + 1)
    tallies = tallies.at[donor].add(-passed).at[receiver].add(passed)
    members = jnp.searchsorted(jnp.cumsum(tallies), jnp.arange(rows * top), side="right").astype(jnp.int32)
    table = members.reshape(top, rows).T
    table = table[jax.random.permutation(jax.random.fold_in(own, 1), rows)]
    offset_by = jax.random.randint(jax.random.fold_in(own, 2), (rows, 1), 0, top)
    return jnp.take_along_axis(table, (jnp.arange(top)[None, :] + offset_by) % top, axis=1)


def portions_of(count, total, most, lean, full):
    loads = [(1 << 20) // math.isqrt(grade ** lean) + 1 for grade in range(1, count + 1)]
    largest = most if full else min(most, max(-(-total // count), total * loads[0] // sum(loads)))
    least = 1 if total - largest >= count - 1 else 0
    given, rest = [largest] + [least] * (count - 1), total - largest - least * (count - 1)
    while rest > 0:
        free = [i for i in range(1, count) if given[i] < largest] or [i for i in range(1, count) if given[i] < most]
        pool, budget = sum([loads[i] for i in free]), rest
        for i in free:
            addition = min(most - given[i], max(1, budget * loads[i] // pool), rest)
            given[i] = given[i] + addition
            rest = rest - addition
    return np.array(given)


def gaussian(stream_key, shape, width, most, shards=(), kind=jnp.bfloat16):
    gain = shard_levels(stream_key, shape, shards, -0.22, 0.18) if shards else 1.0
    entries = jax.random.normal(stream_key, shape, jnp.float32) * width * gain
    return jnp.minimum(jnp.maximum(entries, -most), most).astype(kind)


def setup_inputs(seed: int = 0, part: int = 0) -> dict:
    key_of = jax.random.split(jax.random.key(seed), 12)
    part_keys = jax.random.split(jax.random.fold_in(key_of[11], part), 12)
    moe_input = gaussian(part_keys[0], (TOKENS, D), 1.0, 6.0, ((0, 16),))
    expert_ids_keys = jax.random.split(jax.random.fold_in(part_keys[1], 1), TOKENS // ROWS)
    expert_ids_turns = jax.random.permutation(jax.random.fold_in(part_keys[1], 3), TOKENS // ROWS)
    expert_ids = jax.vmap(lambda own, number: shared_out(jax.random.fold_in(part_keys[1], 2), own, number, ROWS, EXPERTS, TOP, CAP, 2))(expert_ids_keys, expert_ids_turns).reshape((TOKENS, TOP))
    route_scores = jnp.clip(jnp.exp(math.log(1.0) - 2.9957323 * jax.random.uniform(part_keys[2], (TOKENS, TOP), jnp.float32) ** shard_levels(part_keys[2], (TOKENS, TOP), ((0, 16),), -0.2, 0.2)), 0.05, 1.0)
    gate_weight = gaussian(key_of[3], (D, EXPERTS * FFW), D ** -0.5, 0.0625, ((1, 16),))
    up_weight = gaussian(key_of[4], (D, EXPERTS * FFW), D ** -0.5, 0.0625, ((1, 16),))
    down_weight = gaussian(key_of[5], (EXPERTS * FFW, D), FFW ** -0.5, 0.1875, ((0, 16),))
    q_latent = gaussian(part_keys[6], (SEQS, STEPS, HEADS * LATENT), 1.0, 6.0, ((0, 16),))
    q_rope = draw_q_rope(jax.random.fold_in(jax.random.fold_in(key_of[11], part), 71), part)
    latent_cache = gaussian(part_keys[8], (SEQS, LMAX, LATENT), 1.0, 6.0, ((0, 16),))
    rope_cache = draw_rope_cache(jax.random.fold_in(jax.random.fold_in(key_of[11], part), 71), part)
    cache_lengths = draw_cache_lengths(jax.random.fold_in(jax.random.fold_in(key_of[11], part), 71), part)
    return dict(moe_input=moe_input, expert_ids=expert_ids, route_scores=route_scores, gate_weight=gate_weight, up_weight=up_weight, down_weight=down_weight, q_latent=q_latent, q_rope=q_rope, latent_cache=latent_cache, rope_cache=rope_cache, cache_lengths=cache_lengths)


score_factor = 192.0 ** -0.5
route_factor = 2.5


def slot_table(block_ids):
    flat = block_ids.reshape(-1)
    onehot = (flat[:, None] == jnp.arange(EXPERTS, dtype=jnp.int32)[None, :]).astype(jnp.int32)
    before = jnp.cumsum(onehot, axis=0) - onehot
    slot = jnp.sum(before * onehot, axis=1).astype(jnp.int32)
    place = (flat * CAP + slot).astype(jnp.int32)
    source = (jnp.arange(flat.shape[0], dtype=jnp.int32) // TOP + 1).astype(jnp.int32)
    owner = jnp.zeros((EXPERTS * CAP,), jnp.int32).at[place].set(source) - 1
    return place, owner


def fill_slots(block_rows, owner):
    picked = block_rows[jnp.maximum(owner, 0)]
    return jnp.where((owner >= 0)[:, None], picked, jnp.zeros_like(picked))


def reference(moe_input, expert_ids, route_scores, gate_weight, up_weight, down_weight, q_latent, q_rope, latent_cache, rope_cache, cache_lengths):
    block_rows = moe_input.reshape(N_ATTN, ROWS, D)
    block_ids = expert_ids.reshape(N_ATTN, ROWS, TOP)
    places, owners = jax.vmap(slot_table)(block_ids)
    slots = jax.vmap(fill_slots)(block_rows, owners).reshape(N_ATTN, EXPERTS, CAP, D)

    def one_expert(expert):
        token_rows = slots[:, expert].reshape(N_ATTN * CAP, D)
        start = (expert * FFW).astype(jnp.int32)
        gate_cols = lax.dynamic_slice_in_dim(gate_weight, start, FFW, 1)
        up_cols = lax.dynamic_slice_in_dim(up_weight, start, FFW, 1)
        down_rows = lax.dynamic_slice_in_dim(down_weight, start, FFW, 0).reshape(SHARDS, FF_DEV, D)
        gate_part = jnp.dot(token_rows, gate_cols, preferred_element_type=jnp.float32)
        up_part = jnp.dot(token_rows, up_cols, preferred_element_type=jnp.float32)
        hidden = (jax.nn.silu(gate_part) * up_part).astype(jnp.bfloat16)
        hidden = hidden.reshape(N_ATTN * CAP, SHARDS, FF_DEV)
        partial_value = jnp.einsum("rsf,sfd->rsd", hidden.astype(jnp.float32), down_rows.astype(jnp.float32)).astype(jnp.bfloat16)
        summed = jnp.sum(partial_value.astype(jnp.float32), axis=1).astype(jnp.bfloat16)
        return summed.reshape(N_ATTN, CAP, D)

    expert_out = lax.map(one_expert, jnp.arange(EXPERTS, dtype=jnp.int32))
    expert_out = jnp.transpose(expert_out, (1, 0, 2, 3)).reshape(N_ATTN, EXPERTS * CAP, D)
    combine = route_factor * route_scores / jnp.sum(route_scores, axis=1, keepdims=True)
    combine = combine.reshape(N_ATTN, ROWS, TOP)

    def mix_block(block_out, block_place, block_weight):
        values = block_out[block_place].astype(jnp.float32).reshape(ROWS, TOP, D)
        return jnp.sum(values * block_weight[:, :, None], axis=1).astype(jnp.bfloat16)

    moe_output = jax.vmap(mix_block)(expert_out, places, combine).reshape(TOKENS, D)

    query_lat = q_latent.reshape(SEQS, STEPS, HEADS, LATENT).astype(jnp.float32)
    query_rot = q_rope.reshape(SEQS, STEPS, HEADS, ROPE).astype(jnp.float32)
    scores = jnp.einsum("bthc,bpc->bthp", query_lat, latent_cache.astype(jnp.float32))
    scores = scores + jnp.einsum("bthc,bpc->bthp", query_rot, rope_cache.astype(jnp.float32))
    scores = scores * score_factor
    position = jnp.arange(LMAX, dtype=jnp.int32)
    limit = cache_lengths[:, None] - STEPS + jnp.arange(STEPS, dtype=jnp.int32)[None, :]
    allowed = position[None, None, None, :] <= limit[:, :, None, None]
    scores = jnp.where(allowed, scores, -jnp.inf)
    largest = jnp.max(scores, axis=-1, keepdims=True)
    weights = jnp.exp(scores - largest)
    probs = (weights / jnp.sum(weights, axis=-1, keepdims=True)).astype(jnp.bfloat16)
    attn = jnp.einsum("bthp,bpc->bthc", probs.astype(jnp.float32), latent_cache.astype(jnp.float32))
    attn_output = attn.astype(jnp.bfloat16).reshape(SEQS, STEPS, HEADS * LATENT)
    return moe_output, attn_output
```

```python
import functools

import jax
import jax.numpy as jnp
from jax import lax
from jax.experimental import pallas as pl
from jax.experimental.pallas import tpu as pltpu
from jax.sharding import PartitionSpec as P

EXPERTS = 8
CAP = 9
SUB = 8
MIB = 1 << 20

score_factor = 192.0 ** (-0.5)
route_factor = 2.5

f32 = jnp.float32
bf16 = jnp.bfloat16


def dot(a, b):
    return jnp.dot(a, b, preferred_element_type=f32)


def dot_t(a, b):
    return lax.dot_general(a, b, (((0,), (0,)), ((), ())), preferred_element_type=f32)


def routing(ids, chip):
    rows = ids.shape[0]
    col = lax.broadcasted_iota(jnp.int32, (rows, EXPERTS * SUB), 1)
    expert = jnp.bitwise_xor(col // SUB, chip)
    first = ids[:, 0:1] == expert
    hit = first | (ids[:, 1:2] == expert)
    r = lax.broadcasted_iota(jnp.int32, (rows, rows), 0)
    c = lax.broadcasted_iota(jnp.int32, (rows, rows), 1)
    slot = dot((c < r).astype(f32).astype(bf16), hit.astype(f32).astype(bf16)).astype(jnp.int32)
    return hit, slot, first, col % SUB


def pack_kernel(chip_ref, ids_ref, x_ref, *outs):
    features = x_ref.shape[1]
    tail = features // SUB
    hit, slot, _, s = routing(ids_ref[...], chip_ref[0])
    zero = jnp.zeros(hit.shape, f32)
    pick = jnp.where(hit & (slot == s), 1.0, zero).astype(bf16)
    main = dot_t(pick, x_ref[...]).astype(bf16)
    last = jnp.zeros((EXPERTS * SUB, tail), f32)
    for i in range(SUB):
        pick = jnp.where(hit & (slot == SUB) & (s == i), 1.0, zero).astype(bf16)
        last = last + dot_t(pick, x_ref[:, i * tail:(i + 1) * tail])
    last = last.astype(bf16)
    for m, out in enumerate(outs):
        out[:, :features] = main[m * SUB:(m + 1) * SUB]
        out[:, features:] = last[m * SUB:(m + 1) * SUB]


def pack(chip, ids, x):
    features = x.shape[1]
    wide = features + features // SUB
    return pl.pallas_call(
        pack_kernel,
        out_shape=[jax.ShapeDtypeStruct((SUB, wide), bf16)] * EXPERTS,
        in_specs=[pl.BlockSpec(memory_space=pltpu.SMEM)] + [pl.BlockSpec(memory_space=pltpu.VMEM)] * 2,
        out_specs=[pl.BlockSpec(memory_space=pltpu.VMEM)] * EXPERTS,
        compiler_params=pltpu.CompilerParams(vmem_limit_bytes=12 * MIB),
        name="pack",
    )(chip, ids, x)


def spread(i, count):
    j = lax.broadcasted_iota(jnp.int32, (count, count * SUB), 0)
    c = lax.broadcasted_iota(jnp.int32, (count, count * SUB), 1)
    return jnp.where(c == j * SUB + i, 1.0, jnp.zeros((count, count * SUB), f32)).astype(bf16)


def expert_kernel(count, *refs):
    ins, (gate_ref, up_ref, down_ref) = refs[:count], refs[count:count + 3]
    outs, (rows_ref, tail_ref, acc_ref) = refs[count + 3:2 * count + 3], refs[2 * count + 3:]
    features, units = gate_ref.shape
    tail = features // SUB
    top = count * SUB
    for j, ref in enumerate(ins):
        rows_ref[j * SUB:(j + 1) * SUB, :] = ref[:, :features]
        tail_ref[j * SUB:(j + 1) * SUB, :] = ref[:, features:]
    folded = tail_ref[...]
    for i in range(SUB):
        rows_ref[top:, i * tail:(i + 1) * tail] = dot(spread(i, count), folded).astype(bf16)
    acc_ref[...] = jnp.zeros_like(acc_ref)
    step = 1024

    def contract(k, carry):
        at = pl.ds(pl.multiple_of(k * step, step), step)
        a = rows_ref[:, at]
        acc_ref[:, :units] += dot(a, gate_ref[at, :])
        acc_ref[:, units:] += dot(a, up_ref[at, :])
        return carry

    lax.fori_loop(0, features // step, contract, 0)
    hidden = (jax.nn.silu(acc_ref[:, :units]) * acc_ref[:, units:]).astype(bf16)
    folded = jnp.zeros((top, tail), f32)
    for k in range(SUB // 2):
        part = dot(hidden, down_ref[:, 2 * k * tail:2 * (k + 1) * tail]).astype(bf16)
        for j, out in enumerate(outs):
            out[:, 2 * k * tail:2 * (k + 1) * tail] = part[j * SUB:(j + 1) * SUB]
        folded = folded + dot_t(spread(2 * k, count), part[top:, :tail])
        folded = folded + dot_t(spread(2 * k + 1, count), part[top:, tail:])
    folded = folded.astype(bf16)
    for j, out in enumerate(outs):
        out[:, features:] = folded[j * SUB:(j + 1) * SUB]


def experts(buffers, gate_weight, up_weight, down_weight):
    count = len(buffers)
    features, units = gate_weight.shape
    vmem = pl.BlockSpec(memory_space=pltpu.VMEM)
    return pl.pallas_call(
        functools.partial(expert_kernel, count),
        out_shape=[jax.ShapeDtypeStruct(buffers[0].shape, bf16)] * count,
        in_specs=[vmem] * (count + 3),
        out_specs=[vmem] * count,
        scratch_shapes=[
            pltpu.VMEM((count * CAP, features), bf16),
            pltpu.VMEM((count * SUB, features // SUB), bf16),
            pltpu.VMEM((count * CAP, 2 * units), f32),
        ],
        compiler_params=pltpu.CompilerParams(vmem_limit_bytes=36 * MIB),
        name="experts",
    )(*buffers, gate_weight, up_weight, down_weight)


def combine_kernel(chip_ref, ids_ref, scores_ref, *refs):
    ins, out_ref, (rows_ref, tail_ref) = refs[:EXPERTS], refs[EXPERTS], refs[EXPERTS + 1:]
    features = out_ref.shape[1]
    tail = features // SUB
    hit, slot, first, s = routing(ids_ref[...], chip_ref[0])
    scores = scores_ref[...]
    weight = route_factor * scores / (scores[:, 0:1] + scores[:, 1:2])
    weight = jnp.where(first, weight[:, 0:1], weight[:, 1:2])
    zero = jnp.zeros(hit.shape, f32)
    for m, ref in enumerate(ins):
        rows_ref[m * SUB:(m + 1) * SUB, :] = ref[:, :features]
        tail_ref[m * SUB:(m + 1) * SUB, :] = ref[:, features:]

    def parts(mask):
        w = jnp.where(mask, weight, zero)
        high = w.astype(bf16)
        return high, (w - high.astype(f32)).astype(bf16)

    high, low = parts(hit & (slot == s))
    folded = tail_ref[...]
    for i in range(SUB):
        at = slice(i * tail, (i + 1) * tail)
        last_high, last_low = parts(hit & (slot == SUB) & (s == i))
        total = dot(high, rows_ref[:, at]) + dot(low, rows_ref[:, at])
        total = total + dot(last_high, folded) + dot(last_low, folded)
        out_ref[:, at] = total.astype(bf16)


def combine(chip, ids, scores, buffers, features):
    vmem = pl.BlockSpec(memory_space=pltpu.VMEM)
    return pl.pallas_call(
        combine_kernel,
        out_shape=jax.ShapeDtypeStruct((ids.shape[0], features), bf16),
        in_specs=[pl.BlockSpec(memory_space=pltpu.SMEM)] + [vmem] * (2 + EXPERTS),
        out_specs=vmem,
        scratch_shapes=[
            pltpu.VMEM((EXPERTS * SUB, features), bf16),
            pltpu.VMEM((EXPERTS * SUB, features // SUB), bf16),
        ],
        compiler_params=pltpu.CompilerParams(vmem_limit_bytes=12 * MIB),
        name="combine",
    )(chip, ids, scores, *buffers)


def moe_by_chips(moe_input, expert_ids, route_scores, gate_weight, up_weight, down_weight):
    features = moe_input.shape[1]
    members = lax.axis_size("attn")
    chip = (lax.axis_index("attn") // 2).astype(jnp.int32).reshape(1)

    def across(value, m):
        return lax.ppermute(value, "attn", [(i, i ^ (2 * m)) for i in range(members)])

    def sibling(value):
        return lax.ppermute(value, "attn", [(i, i ^ 1) for i in range(members)])

    sent = pack(chip, expert_ids, moe_input)
    mine = [sent[0]] + [across(sent[m], m) for m in range(1, EXPERTS)]
    theirs = [sibling(value) for value in mine]
    partial = experts(mine + theirs, gate_weight, up_weight, down_weight)
    other = [sibling(value) for value in partial[EXPERTS:]]
    total = [(a.astype(f32) + b.astype(f32)).astype(bf16) for a, b in zip(partial[:EXPERTS], other)]
    back = [total[0]] + [across(total[m], m) for m in range(1, EXPERTS)]
    return combine(chip, expert_ids, route_scores, back, features)


def slot_table(block_ids):
    flat = block_ids.reshape(-1)
    picks = block_ids.shape[1]
    count = flat.shape[0]
    onehot = (flat[:, None] == jnp.arange(EXPERTS, dtype=jnp.int32)[None, :]).astype(jnp.int32)
    earlier = jnp.arange(count)[:, None] > jnp.arange(count)[None, :]
    same = flat[:, None] == flat[None, :]
    slot = jnp.sum((earlier & same).astype(jnp.int32), axis=1)
    place = flat * CAP + slot
    source = jnp.arange(count, dtype=jnp.int32) // picks + 1
    owner = jnp.zeros((EXPERTS * CAP,), jnp.int32).at[place].set(source) - 1
    return (place, owner)


def expert_rows(received, gate_weight, up_weight, down_weight):
    features = received.shape[-1]
    flat_rows = received.reshape(-1, features)
    gate_part = jnp.dot(flat_rows, gate_weight, preferred_element_type=jnp.float32)
    up_part = jnp.dot(flat_rows, up_weight, preferred_element_type=jnp.float32)
    hidden = (jax.nn.silu(gate_part) * up_part).astype(jnp.bfloat16)
    partial_value = jnp.dot(hidden, down_weight, preferred_element_type=jnp.float32)
    return partial_value.astype(jnp.bfloat16).reshape(received.shape)


def moe_by_slots(moe_input, expert_ids, route_scores, gate_weight, up_weight, down_weight):
    members = lax.axis_size("attn")
    shards = members // EXPERTS
    features = moe_input.shape[1]
    place, owner = slot_table(expert_ids)
    picked = moe_input[jnp.maximum(owner, 0)]
    slot_rows = jnp.where((owner >= 0)[:, None], picked, jnp.zeros_like(picked))
    outbound = jnp.broadcast_to(
        slot_rows.reshape(EXPERTS, 1, CAP, features), (EXPERTS, shards, CAP, features)
    )
    outbound = outbound.reshape(members, CAP, features)
    partial_value = expert_rows(
        lax.all_to_all(outbound, "attn", split_axis=0, concat_axis=0, tiled=True),
        gate_weight,
        up_weight,
        down_weight,
    )
    returned = lax.all_to_all(partial_value, "attn", split_axis=0, concat_axis=0, tiled=True)
    grouped = returned.reshape((EXPERTS, shards) + returned.shape[1:]).astype(jnp.float32)
    expert_out = jnp.sum(grouped, axis=1).astype(jnp.bfloat16)
    combine_weight = route_factor * route_scores / jnp.sum(route_scores, axis=1, keepdims=True)
    token_count, picks = expert_ids.shape
    values = expert_out.reshape(EXPERTS * CAP, features)[place].astype(jnp.float32)
    values = values.reshape(token_count, picks, features)
    return jnp.sum(values * combine_weight[:, :, None], axis=1).astype(jnp.bfloat16)


def attend(q_latent, q_rope, latent_cache, rope_cache, cache_lengths):
    seq_count, step_count, _ = q_latent.shape
    cache_len = latent_cache.shape[1]
    latent_width = latent_cache.shape[2]
    rope_width = rope_cache.shape[2]
    head_count = q_latent.shape[2] // latent_width
    query_lat = q_latent.reshape(seq_count, step_count, head_count, latent_width)
    query_rot = q_rope.reshape(seq_count, step_count, head_count, rope_width)
    scores = jnp.einsum(
        "bthc,bpc->bthp", query_lat, latent_cache, preferred_element_type=jnp.float32
    )
    scores = scores + jnp.einsum(
        "bthc,bpc->bthp", query_rot, rope_cache, preferred_element_type=jnp.float32
    )
    scores = scores * score_factor
    position = jnp.arange(cache_len, dtype=jnp.int32)
    limit = cache_lengths[:, None] - step_count + jnp.arange(step_count, dtype=jnp.int32)[None, :]
    allowed = position[None, None, None, :] <= limit[:, :, None, None]
    scores = jnp.where(allowed, scores, -jnp.inf)
    largest = jnp.max(scores, axis=-1, keepdims=True)
    weights = jnp.exp(scores - largest)
    probs = (weights / jnp.sum(weights, axis=-1, keepdims=True)).astype(jnp.bfloat16)
    attn = jnp.einsum("bthp,bpc->bthc", probs, latent_cache, preferred_element_type=jnp.float32)
    return attn.astype(jnp.bfloat16).reshape(seq_count, step_count, head_count * latent_width)


def body(
    moe_input,
    expert_ids,
    route_scores,
    gate_weight,
    up_weight,
    down_weight,
    q_latent,
    q_rope,
    latent_cache,
    rope_cache,
    cache_lengths,
):
    moe = moe_by_chips if lax.axis_size("attn") == 2 * EXPERTS else moe_by_slots
    moe_output = moe(moe_input, expert_ids, route_scores, gate_weight, up_weight, down_weight)
    attn_output = attend(q_latent, q_rope, latent_cache, rope_cache, cache_lengths)
    return (moe_output, attn_output)


def solution(mesh):
    placed = (
        P(("rep", "attn"), None),
        P(("rep", "attn"), None),
        P(("rep", "attn"), None),
        P(None, "attn"),
        P(None, "attn"),
        P("attn", None),
        P(("rep", "attn"), None, None),
        P(("rep", "attn"), None, None),
        P(("rep", "attn"), None, None),
        P(("rep", "attn"), None, None),
        P(("rep", "attn")),
    )
    return jax.shard_map(
        body,
        mesh=mesh,
        in_specs=placed,
        out_specs=(P(("rep", "attn"), None), P(("rep", "attn"), None, None)),
        check_vma=False,
    )
```

```python
import functools

import jax
import jax.numpy as jnp
from jax import lax
from jax.experimental import pallas as pl
from jax.experimental.pallas import tpu as pltpu
from jax.sharding import PartitionSpec as P

EXPERTS = 8
CAP = 9
SUB = 8
FOLD = SUB // 2
MIB = 1 << 20
ORDER = (7, 6, 5, 4, 3, 2, 1)
VMEM = pl.BlockSpec(memory_space=pltpu.VMEM)

score_factor = 192.0 ** (-0.5)
route_factor = 2.5

f32 = jnp.float32
bf16 = jnp.bfloat16


def dot(a, b):
    return jnp.dot(a, b, preferred_element_type=f32)


def dot_t(a, b):
    return lax.dot_general(a, b, (((0,), (0,)), ((), ())), preferred_element_type=f32)


def routing(ids, chip):
    rows = ids.shape[1]
    shape = (EXPERTS * SUB, rows)
    at = lax.broadcasted_iota(jnp.int32, shape, 0)
    expert = jnp.bitwise_xor(at // SUB, chip)
    first = ids[0:1, :] == expert
    hit = first | (ids[1:2, :] == expert)
    r = lax.broadcasted_iota(jnp.int32, (rows, rows), 0)
    c = lax.broadcasted_iota(jnp.int32, (rows, rows), 1)
    slot = dot(hit.astype(f32).astype(bf16), (r < c).astype(f32).astype(bf16)).astype(jnp.int32)
    return hit, slot, first, at % SUB


def ones(mask):
    return jnp.where(mask, 1.0, jnp.zeros(mask.shape, f32)).astype(bf16)


def pack_kernel(chip_ref, ids_ref, x_ref, *outs):
    features = x_ref.shape[1]
    tail = features // SUB
    hit, slot, _, q = routing(ids_ref[...], chip_ref[0])
    main = dot(ones(hit & (slot == q)), x_ref[...]).astype(bf16)
    last = jnp.zeros((EXPERTS * SUB, tail), f32)
    for i in range(SUB):
        last = last + dot(ones(hit & (slot == SUB) & (q == i)), x_ref[:, i * tail:(i + 1) * tail])
    last = last.astype(bf16)
    for m, out in enumerate(outs):
        out[:, :features] = main[m * SUB:(m + 1) * SUB]
        out[:, features:] = last[m * SUB:(m + 1) * SUB]


def pack(chip, ids, x):
    features = x.shape[1]
    return pl.pallas_call(
        pack_kernel,
        out_shape=[jax.ShapeDtypeStruct((SUB, features + features // SUB), bf16)] * EXPERTS,
        in_specs=[pl.BlockSpec(memory_space=pltpu.SMEM)] + [VMEM] * 2,
        out_specs=[VMEM] * EXPERTS,
        compiler_params=pltpu.CompilerParams(vmem_limit_bytes=12 * MIB),
        name="pack",
    )(chip, ids, x)


def spread(i, count):
    j = lax.broadcasted_iota(jnp.int32, (count, count * SUB), 0)
    c = lax.broadcasted_iota(jnp.int32, (count, count * SUB), 1)
    return ones(c == j * SUB + i)


def expert_kernel(groups, *refs):
    ins, (gate_hbm, up_hbm, down_hbm) = refs[:groups], refs[groups:groups + 3]
    mine_ref, theirs_ref = refs[groups + 3:groups + 5]
    gate_ref, up_ref, down_ref, rows_ref, tail_ref, acc_ref, sems = refs[groups + 5:]
    features, units = gate_ref.shape
    tail = features // SUB
    top = tail_ref.shape[0]
    count = top // SUB
    wide = 2 * tail
    copies = []
    for k in range(FOLD):
        rows = pl.ds(k * wide, wide)
        for ref, to in ((gate_hbm, gate_ref), (up_hbm, up_ref)):
            copies.append(pltpu.make_async_copy(ref.at[rows], to.at[rows], sems.at[len(copies)]))
    for k in range(FOLD):
        columns = pl.ds(k * wide, wide)
        copies.append(pltpu.make_async_copy(down_hbm.at[:, columns], down_ref.at[:, columns], sems.at[len(copies)]))
    for copy in copies:
        copy.start()
    start = 0
    for ref in ins:
        rows = slice(start, start + ref.shape[0])
        rows_ref[rows, :] = ref[:, :features]
        tail_ref[rows, :] = ref[:, features:]
        start += ref.shape[0]
    folded = tail_ref[...]
    for i in range(SUB):
        rows_ref[top:, i * tail:(i + 1) * tail] = dot(spread(i, count), folded).astype(bf16)
    for k in range(FOLD):
        at = slice(k * wide, (k + 1) * wide)
        for n, ref in enumerate((gate_ref, up_ref)):
            copies[2 * k + n].wait()
            columns = slice(n * units, (n + 1) * units)
            product = dot(rows_ref[:, at], ref[at, :])
            acc_ref[:, columns] = product if k == 0 else acc_ref[:, columns] + product
    hidden = (jax.nn.silu(acc_ref[:, :units]) * acc_ref[:, units:]).astype(bf16)
    folded = jnp.zeros((top, tail), f32)
    for k in range(FOLD):
        copies[2 * FOLD + k].wait()
        at = slice(k * wide, (k + 1) * wide)
        part = dot(hidden, down_ref[:, at]).astype(bf16)
        mine_ref[:, at] = part[:top // 2]
        theirs_ref[:, at] = part[top // 2:top]
        folded = folded + dot_t(spread(2 * k, count), part[top:, :tail])
        folded = folded + dot_t(spread(2 * k + 1, count), part[top:, tail:])
    folded = folded.astype(bf16)
    mine_ref[:, features:] = folded[:top // 2]
    theirs_ref[:, features:] = folded[top // 2:]


def experts(groups, gate_weight, up_weight, down_weight):
    features, units = gate_weight.shape
    top = sum(group.shape[0] for group in groups)
    rows = top + top // SUB
    wide = groups[0].shape[1]
    return pl.pallas_call(
        functools.partial(expert_kernel, len(groups)),
        out_shape=[jax.ShapeDtypeStruct((top // 2, wide), bf16)] * 2,
        in_specs=[VMEM] * len(groups) + [pl.BlockSpec(memory_space=pltpu.HBM)] * 3,
        out_specs=[VMEM] * 2,
        scratch_shapes=[
            pltpu.VMEM(gate_weight.shape, bf16),
            pltpu.VMEM(up_weight.shape, bf16),
            pltpu.VMEM(down_weight.shape, bf16),
            pltpu.VMEM((rows, features), bf16),
            pltpu.VMEM((top, features // SUB), bf16),
            pltpu.VMEM((rows, 2 * units), f32),
            pltpu.SemaphoreType.DMA((3 * FOLD,)),
        ],
        compiler_params=pltpu.CompilerParams(vmem_limit_bytes=36 * MIB),
        cost_estimate=pl.CostEstimate(
            flops=6 * rows * features * units, bytes_accessed=6 * features * units, transcendentals=0
        ),
        name="experts",
    )(*groups, gate_weight, up_weight, down_weight)


def add_kernel(a_ref, b_ref, *outs):
    for m, out in enumerate(outs):
        rows = slice(m * SUB, (m + 1) * SUB)
        out[...] = (a_ref[rows, :].astype(f32) + b_ref[rows, :].astype(f32)).astype(bf16)


def add(a, b):
    return pl.pallas_call(
        add_kernel,
        out_shape=[jax.ShapeDtypeStruct((SUB, a.shape[1]), bf16)] * EXPERTS,
        in_specs=[VMEM] * 2,
        out_specs=[VMEM] * EXPERTS,
        compiler_params=pltpu.CompilerParams(vmem_limit_bytes=6 * MIB),
        name="add",
    )(a, b)


def combine_kernel(chip_ref, ids_ref, scores_ref, *refs):
    ins, out_ref, rows_ref = refs[:EXPERTS], refs[EXPERTS], refs[EXPERTS + 1]
    features = out_ref.shape[1]
    tail = features // SUB
    hit, slot, first, q = routing(ids_ref[...], chip_ref[0])
    scores = scores_ref[...]
    weight = route_factor * scores / (scores[0:1, :] + scores[1:2, :])
    weight = jnp.where(first, weight[0:1, :], weight[1:2, :])
    for m, ref in zip(ORDER + (0,), ins):
        rows_ref[m * SUB:(m + 1) * SUB, :] = ref[...]

    def weighted(mask, values):
        w = jnp.where(mask, weight, jnp.zeros_like(weight))
        high = w.astype(bf16)
        low = (w - high.astype(f32)).astype(bf16)
        return dot_t(high, values) + dot_t(low, values)

    folded = rows_ref[:, features:]
    for i in range(SUB):
        at = slice(i * tail, (i + 1) * tail)
        total = weighted(hit & (slot == q), rows_ref[:, at])
        total = total + weighted(hit & (slot == SUB) & (q == i), folded)
        out_ref[:, at] = total.astype(bf16)


def combine(chip, ids, scores, buffers, features):
    return pl.pallas_call(
        combine_kernel,
        out_shape=jax.ShapeDtypeStruct((ids.shape[1], features), bf16),
        in_specs=[pl.BlockSpec(memory_space=pltpu.SMEM)] + [VMEM] * (2 + EXPERTS),
        out_specs=VMEM,
        scratch_shapes=[pltpu.VMEM((EXPERTS * SUB, features + features // SUB), bf16)],
        compiler_params=pltpu.CompilerParams(vmem_limit_bytes=12 * MIB),
        name="combine",
    )(chip, ids, scores, *buffers)


def after(values, *others):
    return lax.optimization_barrier((values, others))[0]


def moe_by_chips(moe_input, expert_ids, route_scores, gate_weight, up_weight, down_weight, attention):
    features = moe_input.shape[1]
    members = lax.axis_size("attn")
    chip = (lax.axis_index("attn") // 2).astype(jnp.int32).reshape(1)
    ids, scores = expert_ids.T, route_scores.T
    weights = [
        pltpu.with_memory_space_constraint(w, pltpu.HBM) for w in (gate_weight, up_weight, down_weight)
    ]
    probs, finish = attention

    def sibling(value):
        return lax.ppermute(value, "attn", [(i, i ^ 1) for i in range(members)])

    def exchange(sent):
        got = {0: sent[0]}
        for m in ORDER:
            got[m] = lax.ppermute(sent[m], "attn", [(i, i ^ (2 * m)) for i in range(members)])
        return got

    got = exchange(pack(chip, ids, moe_input))
    order = (0,) + ORDER[FOLD:] + ORDER[:FOLD]
    first = jnp.concatenate([got[m] for m in order[:FOLD]], axis=0)
    second = jnp.concatenate([got[m] for m in order[FOLD:]], axis=0)
    second = after(second, probs)
    mine, theirs = experts([first, second, sibling(first), sibling(second)], *weights)
    total = add(mine, sibling(theirs))
    attn_output = finish(after(probs, *total))
    back = exchange({m: total[place] for place, m in enumerate(order)})
    moe_output = combine(chip, ids, scores, [back[m] for m in ORDER + (0,)], features)
    return moe_output, attn_output


def slot_table(block_ids):
    flat = block_ids.reshape(-1)
    picks = block_ids.shape[1]
    count = flat.shape[0]
    onehot = (flat[:, None] == jnp.arange(EXPERTS, dtype=jnp.int32)[None, :]).astype(jnp.int32)
    earlier = jnp.arange(count)[:, None] > jnp.arange(count)[None, :]
    same = flat[:, None] == flat[None, :]
    slot = jnp.sum((earlier & same).astype(jnp.int32), axis=1)
    place = flat * CAP + slot
    source = jnp.arange(count, dtype=jnp.int32) // picks + 1
    owner = jnp.zeros((EXPERTS * CAP,), jnp.int32).at[place].set(source) - 1
    return (place, owner)


def expert_rows(received, gate_weight, up_weight, down_weight):
    features = received.shape[-1]
    flat_rows = received.reshape(-1, features)
    gate_part = jnp.dot(flat_rows, gate_weight, preferred_element_type=jnp.float32)
    up_part = jnp.dot(flat_rows, up_weight, preferred_element_type=jnp.float32)
    hidden = (jax.nn.silu(gate_part) * up_part).astype(jnp.bfloat16)
    partial_value = jnp.dot(hidden, down_weight, preferred_element_type=jnp.float32)
    return partial_value.astype(jnp.bfloat16).reshape(received.shape)


def moe_by_slots(moe_input, expert_ids, route_scores, gate_weight, up_weight, down_weight, attention):
    members = lax.axis_size("attn")
    shards = members // EXPERTS
    features = moe_input.shape[1]
    place, owner = slot_table(expert_ids)
    picked = moe_input[jnp.maximum(owner, 0)]
    slot_rows = jnp.where((owner >= 0)[:, None], picked, jnp.zeros_like(picked))
    outbound = jnp.broadcast_to(
        slot_rows.reshape(EXPERTS, 1, CAP, features), (EXPERTS, shards, CAP, features)
    )
    outbound = outbound.reshape(members, CAP, features)
    partial_value = expert_rows(
        lax.all_to_all(outbound, "attn", split_axis=0, concat_axis=0, tiled=True),
        gate_weight,
        up_weight,
        down_weight,
    )
    returned = lax.all_to_all(partial_value, "attn", split_axis=0, concat_axis=0, tiled=True)
    grouped = returned.reshape((EXPERTS, shards) + returned.shape[1:]).astype(jnp.float32)
    expert_out = jnp.sum(grouped, axis=1).astype(jnp.bfloat16)
    combine_weight = route_factor * route_scores / jnp.sum(route_scores, axis=1, keepdims=True)
    token_count, picks = expert_ids.shape
    values = expert_out.reshape(EXPERTS * CAP, features)[place].astype(jnp.float32)
    values = values.reshape(token_count, picks, features)
    moe_output = jnp.sum(values * combine_weight[:, :, None], axis=1).astype(jnp.bfloat16)
    probs, finish = attention
    return moe_output, finish(probs)


def attend(q_latent, q_rope, latent_cache, rope_cache, cache_lengths):
    seq_count, step_count, _ = q_latent.shape
    cache_len = latent_cache.shape[1]
    latent_width = latent_cache.shape[2]
    rope_width = rope_cache.shape[2]
    head_count = q_latent.shape[2] // latent_width
    query_lat = q_latent.reshape(seq_count, step_count, head_count, latent_width)
    query_rot = q_rope.reshape(seq_count, step_count, head_count, rope_width)
    scores = jnp.einsum(
        "bthc,bpc->bthp", query_lat, latent_cache, preferred_element_type=jnp.float32
    )
    scores = scores + jnp.einsum(
        "bthc,bpc->bthp", query_rot, rope_cache, preferred_element_type=jnp.float32
    )
    scores = scores * score_factor
    position = jnp.arange(cache_len, dtype=jnp.int32)
    limit = cache_lengths[:, None] - step_count + jnp.arange(step_count, dtype=jnp.int32)[None, :]
    allowed = position[None, None, None, :] <= limit[:, :, None, None]
    scores = jnp.where(allowed, scores, -jnp.inf)
    largest = jnp.max(scores, axis=-1, keepdims=True)
    weights = jnp.exp(scores - largest)
    probs = (weights / jnp.sum(weights, axis=-1, keepdims=True)).astype(jnp.bfloat16)

    def finish(probs):
        attn = jnp.einsum("bthp,bpc->bthc", probs, latent_cache, preferred_element_type=jnp.float32)
        return attn.astype(jnp.bfloat16).reshape(seq_count, step_count, head_count * latent_width)

    return probs, finish


def body(
    moe_input,
    expert_ids,
    route_scores,
    gate_weight,
    up_weight,
    down_weight,
    q_latent,
    q_rope,
    latent_cache,
    rope_cache,
    cache_lengths,
):
    moe = moe_by_chips if lax.axis_size("attn") == 2 * EXPERTS else moe_by_slots
    attention = attend(q_latent, q_rope, latent_cache, rope_cache, cache_lengths)
    return moe(moe_input, expert_ids, route_scores, gate_weight, up_weight, down_weight, attention)


def solution(mesh):
    placed = (
        P(("rep", "attn"), None),
        P(("rep", "attn"), None),
        P(("rep", "attn"), None),
        P(None, "attn"),
        P(None, "attn"),
        P("attn", None),
        P(("rep", "attn"), None, None),
        P(("rep", "attn"), None, None),
        P(("rep", "attn"), None, None),
        P(("rep", "attn"), None, None),
        P(("rep", "attn")),
    )
    return jax.shard_map(
        body,
        mesh=mesh,
        in_specs=placed,
        out_specs=(P(("rep", "attn"), None), P(("rep", "attn"), None, None)),
        check_vma=False,
    )
```

```python
import functools

import jax
import jax.numpy as jnp
from jax import lax
from jax.experimental import pallas as pl
from jax.experimental.pallas import tpu as pltpu
from jax.sharding import PartitionSpec as P

EXPERTS = 8
CAP = 9
SUB = 8
FOLD = SUB // 2
MIB = 1 << 20
ORDER = (7, 6, 5, 1, 2, 4, 3)
GROUPED = (7, 6, 5, 4, 0, 1, 2, 3)
BACK = (7, 6, 5, 4, 3, 2, 1, 0)
HBM = pl.BlockSpec(memory_space=pltpu.HBM)
VMEM = pl.BlockSpec(memory_space=pltpu.VMEM)

score_factor = 192.0 ** (-0.5)
route_factor = 2.5

f32 = jnp.float32
bf16 = jnp.bfloat16


def dot(a, b):
    return jnp.dot(a, b, preferred_element_type=f32)


def dot_t(a, b):
    return lax.dot_general(a, b, (((0,), (0,)), ((), ())), preferred_element_type=f32)


def routing(ids, chip):
    rows = ids.shape[1]
    shape = (EXPERTS * SUB, rows)
    at = lax.broadcasted_iota(jnp.int32, shape, 0)
    expert = jnp.bitwise_xor(at // SUB, chip)
    first = ids[0:1, :] == expert
    hit = first | (ids[1:2, :] == expert)
    r = lax.broadcasted_iota(jnp.int32, (rows, rows), 0)
    c = lax.broadcasted_iota(jnp.int32, (rows, rows), 1)
    slot = dot(hit.astype(f32).astype(bf16), (r < c).astype(f32).astype(bf16)).astype(jnp.int32)
    return hit, slot, first, at % SUB


def ones(mask):
    return jnp.where(mask, 1.0, jnp.zeros(mask.shape, f32)).astype(bf16)


def in_hbm(value):
    return pltpu.with_memory_space_constraint(value, pltpu.HBM)


def pack_kernel(chip_ref, ids_hbm, x_hbm, *refs):
    outs, (ids_ref, x_ref, sems) = refs[:EXPERTS], refs[EXPERTS:]
    ids_copy = pltpu.make_async_copy(ids_hbm, ids_ref, sems.at[0])
    x_copy = pltpu.make_async_copy(x_hbm, x_ref, sems.at[1])
    ids_copy.start()
    x_copy.start()
    ids_copy.wait()
    x_copy.wait()
    features = x_ref.shape[1]
    tail = features // SUB
    hit, slot, _, q = routing(ids_ref[...], chip_ref[0])
    main = dot(ones(hit & (slot == q)), x_ref[...]).astype(bf16)
    last = jnp.zeros((EXPERTS * SUB, tail), f32)
    for i in range(SUB):
        last = last + dot(ones(hit & (slot == SUB) & (q == i)), x_ref[:, i * tail:(i + 1) * tail])
    last = last.astype(bf16)
    for m, out in enumerate(outs):
        out[:, :features] = main[m * SUB:(m + 1) * SUB]
        out[:, features:] = last[m * SUB:(m + 1) * SUB]


def pack(chip, ids, x):
    features = x.shape[1]
    return pl.pallas_call(
        pack_kernel,
        out_shape=[jax.ShapeDtypeStruct((SUB, features + features // SUB), bf16)] * EXPERTS,
        in_specs=[pl.BlockSpec(memory_space=pltpu.SMEM)] + [HBM] * 2,
        out_specs=[VMEM] * EXPERTS,
        scratch_shapes=[
            pltpu.VMEM(ids.shape, ids.dtype),
            pltpu.VMEM(x.shape, x.dtype),
            pltpu.SemaphoreType.DMA((2,)),
        ],
        compiler_params=pltpu.CompilerParams(vmem_limit_bytes=12 * MIB),
        name="pack",
    )(chip, in_hbm(ids), in_hbm(x))


def spread(i, count):
    j = lax.broadcasted_iota(jnp.int32, (count, count * SUB), 0)
    c = lax.broadcasted_iota(jnp.int32, (count, count * SUB), 1)
    return ones(c == j * SUB + i)


def expert_kernel(groups, *refs):
    ins, (gate_hbm, up_hbm, down_hbm) = refs[:groups], refs[groups:groups + 3]
    mine_ref, theirs_ref = refs[groups + 3:groups + 5]
    gate_ref, up_ref, down_ref, rows_ref, tail_ref, acc_ref, sems = refs[groups + 5:]
    features, units = gate_ref.shape
    tail = features // SUB
    top = tail_ref.shape[0]
    count = top // SUB
    wide = 2 * tail
    copies = []
    for k in range(FOLD):
        rows = pl.ds(k * wide, wide)
        for ref, to in ((gate_hbm, gate_ref), (up_hbm, up_ref)):
            copies.append(pltpu.make_async_copy(ref.at[rows], to.at[rows], sems.at[len(copies)]))
    for k in range(FOLD):
        columns = pl.ds(k * wide, wide)
        copies.append(pltpu.make_async_copy(down_hbm.at[:, columns], down_ref.at[:, columns], sems.at[len(copies)]))
    for copy in copies:
        copy.start()
    start = 0
    for ref in ins:
        rows = slice(start, start + ref.shape[0])
        rows_ref[rows, :] = ref[:, :features]
        tail_ref[rows, :] = ref[:, features:]
        start += ref.shape[0]
    folded = tail_ref[...]
    for i in range(SUB):
        rows_ref[top:, i * tail:(i + 1) * tail] = dot(spread(i, count), folded).astype(bf16)
    for k in range(FOLD):
        at = slice(k * wide, (k + 1) * wide)
        for n, ref in enumerate((gate_ref, up_ref)):
            copies[2 * k + n].wait()
            columns = slice(n * units, (n + 1) * units)
            product = dot(rows_ref[:, at], ref[at, :])
            acc_ref[:, columns] = product if k == 0 else acc_ref[:, columns] + product
    hidden = (jax.nn.silu(acc_ref[:, :units]) * acc_ref[:, units:]).astype(bf16)
    folded = jnp.zeros((top, tail), f32)
    for k in range(FOLD):
        copies[2 * FOLD + k].wait()
        at = slice(k * wide, (k + 1) * wide)
        part = dot(hidden, down_ref[:, at]).astype(bf16)
        mine_ref[:, at] = part[:top // 2]
        theirs_ref[:, at] = part[top // 2:top]
        folded = folded + dot_t(spread(2 * k, count), part[top:, :tail])
        folded = folded + dot_t(spread(2 * k + 1, count), part[top:, tail:])
    folded = folded.astype(bf16)
    mine_ref[:, features:] = folded[:top // 2]
    theirs_ref[:, features:] = folded[top // 2:]


def experts(groups, gate_weight, up_weight, down_weight):
    features, units = gate_weight.shape
    top = sum(group.shape[0] for group in groups)
    rows = top + top // SUB
    wide = groups[0].shape[1]
    return pl.pallas_call(
        functools.partial(expert_kernel, len(groups)),
        out_shape=[jax.ShapeDtypeStruct((top // 2, wide), bf16)] * 2,
        in_specs=[VMEM] * len(groups) + [HBM] * 3,
        out_specs=[VMEM] * 2,
        scratch_shapes=[
            pltpu.VMEM(gate_weight.shape, bf16),
            pltpu.VMEM(up_weight.shape, bf16),
            pltpu.VMEM(down_weight.shape, bf16),
            pltpu.VMEM((rows, features), bf16),
            pltpu.VMEM((top, features // SUB), bf16),
            pltpu.VMEM((rows, 2 * units), f32),
            pltpu.SemaphoreType.DMA((3 * FOLD,)),
        ],
        compiler_params=pltpu.CompilerParams(vmem_limit_bytes=36 * MIB),
        cost_estimate=pl.CostEstimate(
            flops=6 * rows * features * units, bytes_accessed=6 * features * units, transcendentals=0
        ),
        name="experts",
    )(*groups, gate_weight, up_weight, down_weight)


def add_kernel(a_ref, b_ref, *outs):
    for m, out in enumerate(outs):
        rows = slice(m * SUB, (m + 1) * SUB)
        out[...] = (a_ref[rows, :].astype(f32) + b_ref[rows, :].astype(f32)).astype(bf16)


def add(a, b):
    return pl.pallas_call(
        add_kernel,
        out_shape=[jax.ShapeDtypeStruct((SUB, a.shape[1]), bf16)] * EXPERTS,
        in_specs=[VMEM] * 2,
        out_specs=[VMEM] * EXPERTS,
        compiler_params=pltpu.CompilerParams(vmem_limit_bytes=6 * MIB),
        name="add",
    )(a, b)


def combine_kernel(chip_ref, ids_ref, scores_ref, *refs):
    ins, out_ref, rows_ref = refs[:EXPERTS], refs[EXPERTS], refs[EXPERTS + 1]
    features = out_ref.shape[1]
    tail = features // SUB
    hit, slot, first, q = routing(ids_ref[...], chip_ref[0])
    scores = scores_ref[...]
    weight = route_factor * scores / (scores[0:1, :] + scores[1:2, :])
    weight = jnp.where(first, weight[0:1, :], weight[1:2, :])
    for m, ref in zip(BACK, ins):
        rows_ref[m * SUB:(m + 1) * SUB, :] = ref[...]

    def weighted(mask, values):
        w = jnp.where(mask, weight, jnp.zeros_like(weight))
        high = w.astype(bf16)
        low = (w - high.astype(f32)).astype(bf16)
        return dot_t(high, values) + dot_t(low, values)

    folded = rows_ref[:, features:]
    for i in range(SUB):
        at = slice(i * tail, (i + 1) * tail)
        total = weighted(hit & (slot == q), rows_ref[:, at])
        total = total + weighted(hit & (slot == SUB) & (q == i), folded)
        out_ref[:, at] = total.astype(bf16)


def combine(chip, ids, scores, buffers, features):
    return pl.pallas_call(
        combine_kernel,
        out_shape=jax.ShapeDtypeStruct((ids.shape[1], features), bf16),
        in_specs=[pl.BlockSpec(memory_space=pltpu.SMEM)] + [VMEM] * (2 + EXPERTS),
        out_specs=VMEM,
        scratch_shapes=[pltpu.VMEM((EXPERTS * SUB, features + features // SUB), bf16)],
        compiler_params=pltpu.CompilerParams(vmem_limit_bytes=12 * MIB),
        name="combine",
    )(chip, ids, scores, *buffers)


def after(values, *others):
    return lax.optimization_barrier((values, others))[0]


def moe_by_chips(moe_input, expert_ids, route_scores, gate_weight, up_weight, down_weight, attention):
    features = moe_input.shape[1]
    members = lax.axis_size("attn")
    chip = (lax.axis_index("attn") // 2).astype(jnp.int32).reshape(1)
    ids, scores = expert_ids.T, route_scores.T
    weights = [in_hbm(w) for w in (gate_weight, up_weight, down_weight)]
    scores_of, soften, finish = attention

    def sibling(value):
        return lax.ppermute(value, "attn", [(i, i ^ 1) for i in range(members)])

    def exchange(sent, *first):
        got = {0: sent[0]}
        for m in ORDER:
            value = after(sent[m], got[5 - m], *first) if m in (4, 3) else sent[m]
            got[m] = lax.ppermute(value, "attn", [(i, i ^ (2 * m)) for i in range(members)])
        return got

    got = exchange(pack(chip, ids, moe_input))
    order = GROUPED
    first = jnp.concatenate([got[m] for m in order[:FOLD]], axis=0)
    second = jnp.concatenate([got[m] for m in order[FOLD:]], axis=0)
    probs = soften(after(scores_of, got[1]))
    second = after(second, probs)
    mine, theirs = experts([first, second, sibling(first), sibling(second)], *weights)
    total = add(mine, sibling(theirs))
    attn_output = finish(after(probs, *total))
    back = exchange({m: total[place] for place, m in enumerate(order)}, attn_output)
    moe_output = combine(chip, ids, scores, [back[m] for m in BACK], features)
    return moe_output, attn_output


def slot_table(block_ids):
    flat = block_ids.reshape(-1)
    picks = block_ids.shape[1]
    count = flat.shape[0]
    onehot = (flat[:, None] == jnp.arange(EXPERTS, dtype=jnp.int32)[None, :]).astype(jnp.int32)
    earlier = jnp.arange(count)[:, None] > jnp.arange(count)[None, :]
    same = flat[:, None] == flat[None, :]
    slot = jnp.sum((earlier & same).astype(jnp.int32), axis=1)
    place = flat * CAP + slot
    source = jnp.arange(count, dtype=jnp.int32) // picks + 1
    owner = jnp.zeros((EXPERTS * CAP,), jnp.int32).at[place].set(source) - 1
    return (place, owner)


def expert_rows(received, gate_weight, up_weight, down_weight):
    features = received.shape[-1]
    flat_rows = received.reshape(-1, features)
    gate_part = jnp.dot(flat_rows, gate_weight, preferred_element_type=jnp.float32)
    up_part = jnp.dot(flat_rows, up_weight, preferred_element_type=jnp.float32)
    hidden = (jax.nn.silu(gate_part) * up_part).astype(jnp.bfloat16)
    partial_value = jnp.dot(hidden, down_weight, preferred_element_type=jnp.float32)
    return partial_value.astype(jnp.bfloat16).reshape(received.shape)


def moe_by_slots(moe_input, expert_ids, route_scores, gate_weight, up_weight, down_weight, attention):
    members = lax.axis_size("attn")
    shards = members // EXPERTS
    features = moe_input.shape[1]
    place, owner = slot_table(expert_ids)
    picked = moe_input[jnp.maximum(owner, 0)]
    slot_rows = jnp.where((owner >= 0)[:, None], picked, jnp.zeros_like(picked))
    outbound = jnp.broadcast_to(
        slot_rows.reshape(EXPERTS, 1, CAP, features), (EXPERTS, shards, CAP, features)
    )
    outbound = outbound.reshape(members, CAP, features)
    partial_value = expert_rows(
        lax.all_to_all(outbound, "attn", split_axis=0, concat_axis=0, tiled=True),
        gate_weight,
        up_weight,
        down_weight,
    )
    returned = lax.all_to_all(partial_value, "attn", split_axis=0, concat_axis=0, tiled=True)
    grouped = returned.reshape((EXPERTS, shards) + returned.shape[1:]).astype(jnp.float32)
    expert_out = jnp.sum(grouped, axis=1).astype(jnp.bfloat16)
    combine_weight = route_factor * route_scores / jnp.sum(route_scores, axis=1, keepdims=True)
    token_count, picks = expert_ids.shape
    values = expert_out.reshape(EXPERTS * CAP, features)[place].astype(jnp.float32)
    values = values.reshape(token_count, picks, features)
    moe_output = jnp.sum(values * combine_weight[:, :, None], axis=1).astype(jnp.bfloat16)
    scores_of, soften, finish = attention
    return moe_output, finish(soften(scores_of))


def attend(q_latent, q_rope, latent_cache, rope_cache, cache_lengths):
    seq_count, step_count, _ = q_latent.shape
    cache_len = latent_cache.shape[1]
    latent_width = latent_cache.shape[2]
    rope_width = rope_cache.shape[2]
    head_count = q_latent.shape[2] // latent_width
    query_lat = q_latent.reshape(seq_count, step_count, head_count, latent_width)
    query_rot = q_rope.reshape(seq_count, step_count, head_count, rope_width)
    scores = jnp.einsum(
        "bthc,bpc->bthp", query_lat, latent_cache, preferred_element_type=jnp.float32
    )
    scores = scores + jnp.einsum(
        "bthc,bpc->bthp", query_rot, rope_cache, preferred_element_type=jnp.float32
    )

    def soften(scores):
        scores = scores * score_factor
        position = jnp.arange(cache_len, dtype=jnp.int32)
        limit = cache_lengths[:, None] - step_count + jnp.arange(step_count, dtype=jnp.int32)[None, :]
        allowed = position[None, None, None, :] <= limit[:, :, None, None]
        scores = jnp.where(allowed, scores, -jnp.inf)
        largest = jnp.max(scores, axis=-1, keepdims=True)
        weights = jnp.exp(scores - largest)
        return (weights / jnp.sum(weights, axis=-1, keepdims=True)).astype(jnp.bfloat16)

    def finish(probs):
        attn = jnp.einsum("bthp,bpc->bthc", probs, latent_cache, preferred_element_type=jnp.float32)
        return attn.astype(jnp.bfloat16).reshape(seq_count, step_count, head_count * latent_width)

    return scores, soften, finish


def body(
    moe_input,
    expert_ids,
    route_scores,
    gate_weight,
    up_weight,
    down_weight,
    q_latent,
    q_rope,
    latent_cache,
    rope_cache,
    cache_lengths,
):
    moe = moe_by_chips if lax.axis_size("attn") == 2 * EXPERTS else moe_by_slots
    attention = attend(q_latent, q_rope, latent_cache, rope_cache, cache_lengths)
    return moe(moe_input, expert_ids, route_scores, gate_weight, up_weight, down_weight, attention)


def solution(mesh):
    placed = (
        P(("rep", "attn"), None),
        P(("rep", "attn"), None),
        P(("rep", "attn"), None),
        P(None, "attn"),
        P(None, "attn"),
        P("attn", None),
        P(("rep", "attn"), None, None),
        P(("rep", "attn"), None, None),
        P(("rep", "attn"), None, None),
        P(("rep", "attn"), None, None),
        P(("rep", "attn")),
    )
    return jax.shard_map(
        body,
        mesh=mesh,
        in_specs=placed,
        out_specs=(P(("rep", "attn"), None), P(("rep", "attn"), None, None)),
        check_vma=False,
    )
```

```python
import functools

import jax
import jax.numpy as jnp
from jax import lax
from jax.experimental import pallas as pl
from jax.experimental.pallas import tpu as pltpu
from jax.sharding import PartitionSpec as P

EXPERTS = 8
CAP = 9
SUB = 8
FOLD = SUB // 2
MIB = 1 << 20
FAR = (7, 6, 5, 4)
BACK = (7, 6, 5, 1, 2, 3, 4, 0)
PLACED = (0, 1, 2, 3) + FAR
TAKEN = (SUB, SUB, 2 * SUB) + (SUB,) * 4
HBM = pl.BlockSpec(memory_space=pltpu.HBM)
VMEM = pl.BlockSpec(memory_space=pltpu.VMEM)

score_factor = 192.0 ** (-0.5)
route_factor = 2.5

f32 = jnp.float32
bf16 = jnp.bfloat16


def dot(a, b):
    return jnp.dot(a, b, preferred_element_type=f32)


def dot_t(a, b):
    return lax.dot_general(a, b, (((0,), (0,)), ((), ())), preferred_element_type=f32)


def routing(ids, chip):
    rows = ids.shape[1]
    shape = (EXPERTS * SUB, rows)
    at = lax.broadcasted_iota(jnp.int32, shape, 0)
    expert = jnp.bitwise_xor(at // SUB, chip)
    first = ids[0:1, :] == expert
    hit = first | (ids[1:2, :] == expert)
    r = lax.broadcasted_iota(jnp.int32, (rows, rows), 0)
    c = lax.broadcasted_iota(jnp.int32, (rows, rows), 1)
    slot = dot(hit.astype(f32).astype(bf16), (r < c).astype(f32).astype(bf16)).astype(jnp.int32)
    return hit, slot, first, at % SUB


def ones(mask):
    return jnp.where(mask, 1.0, jnp.zeros(mask.shape, f32)).astype(bf16)


def in_hbm(value):
    return pltpu.with_memory_space_constraint(value, pltpu.HBM)


def in_vmem(value):
    return pltpu.with_memory_space_constraint(value, pltpu.VMEM)


def load_kernel(*refs):
    token_ref, sems = refs[-2:]
    token_ref[...] = jnp.zeros_like(token_ref)
    count = len(refs) // 2 - 1
    copies = [pltpu.make_async_copy(refs[i], refs[count + i], sems.at[i]) for i in range(count)]
    for copy in copies:
        copy.start()
    for copy in copies:
        copy.wait()


def load(*weights):
    return pl.pallas_call(
        load_kernel,
        out_shape=[pltpu.VMEM(w.shape, w.dtype) for w in weights] + [jax.ShapeDtypeStruct((8, 128), f32)],
        in_specs=[HBM] * len(weights),
        out_specs=[VMEM] * (len(weights) + 1),
        scratch_shapes=[pltpu.SemaphoreType.DMA((len(weights),))],
        compiler_params=pltpu.CompilerParams(vmem_limit_bytes=MIB),
        name="load",
    )(*[in_hbm(w) for w in weights])


def pack_kernel(chip_ref, ids_ref, x_ref, *outs):
    features = x_ref.shape[1]
    tail = features // SUB
    hit, slot, _, q = routing(ids_ref[...], chip_ref[0])
    main = dot(ones(hit & (slot == q)), x_ref[...]).astype(bf16)
    last = jnp.zeros((EXPERTS * SUB, tail), f32)
    for i in range(SUB):
        last = last + dot(ones(hit & (slot == SUB) & (q == i)), x_ref[:, i * tail:(i + 1) * tail])
    last = last.astype(bf16)
    for m, out in destinations(outs):
        rows = slice(m * SUB, (m + 1) * SUB)
        out[:, :features] = main[rows]
        out[:, features:] = last[rows]


def sent_shapes(wide):
    return [jax.ShapeDtypeStruct((rows, wide), bf16) for rows in (SUB, 2 * SUB) + (SUB,) * 5]


def destinations(outs):
    own, along_y, along_z, *far = outs
    near = [(0, own), (1, along_y.at[:SUB]), (3, along_y.at[SUB:]), (2, along_z)]
    return near + list(zip(FAR, far))


def pack(chip, ids, x):
    features = x.shape[1]
    return pl.pallas_call(
        pack_kernel,
        out_shape=sent_shapes(features + features // SUB),
        in_specs=[pl.BlockSpec(memory_space=pltpu.SMEM)] + [VMEM] * 2,
        out_specs=[VMEM] * len(TAKEN),
        compiler_params=pltpu.CompilerParams(vmem_limit_bytes=12 * MIB),
        name="pack",
    )(chip, in_hbm(ids), in_hbm(x))


def stack_kernel(first_ref, second_ref, out_ref):
    out_ref[:SUB, :] = first_ref[...]
    out_ref[SUB:, :] = second_ref[SUB:, :]


def stack(first, second):
    return pl.pallas_call(
        stack_kernel,
        out_shape=jax.ShapeDtypeStruct(second.shape, bf16),
        in_specs=[VMEM] * 2,
        out_specs=VMEM,
        compiler_params=pltpu.CompilerParams(vmem_limit_bytes=4 * MIB),
        name="stack",
    )(first, second)


def spread(i, count):
    j = lax.broadcasted_iota(jnp.int32, (count, count * SUB), 0)
    c = lax.broadcasted_iota(jnp.int32, (count, count * SUB), 1)
    return ones(c == j * SUB + i)


def expert_kernel(groups, *refs):
    ins, (gate_ref, up_ref, down_ref) = refs[:groups], refs[groups:groups + 3]
    mine_ref, theirs_ref = refs[groups + 3:groups + 5]
    rows_ref, tail_ref, acc_ref = refs[groups + 5:]
    features, units = gate_ref.shape
    tail = features // SUB
    top = tail_ref.shape[0]
    count = top // SUB
    wide = 2 * tail
    start = 0
    for ref, taken in zip(ins, 2 * TAKEN):
        rows = slice(start, start + taken)
        rows_ref[rows, :] = ref[:taken, :features]
        tail_ref[rows, :] = ref[:taken, features:]
        start += taken
    folded = tail_ref[...]
    for i in range(SUB):
        rows_ref[top:, i * tail:(i + 1) * tail] = dot(spread(i, count), folded).astype(bf16)
    for k in range(FOLD):
        at = slice(k * wide, (k + 1) * wide)
        for n, ref in enumerate((gate_ref, up_ref)):
            columns = slice(n * units, (n + 1) * units)
            product = dot(rows_ref[:, at], ref[at, :])
            acc_ref[:, columns] = product if k == 0 else acc_ref[:, columns] + product
    hidden = (jax.nn.silu(acc_ref[:, :units]) * acc_ref[:, units:]).astype(bf16)
    folded = jnp.zeros((top, tail), f32)
    for k in range(FOLD):
        at = slice(k * wide, (k + 1) * wide)
        part = dot(hidden, down_ref[:, at]).astype(bf16)
        mine_ref[:, at] = part[:top // 2]
        theirs_ref[:, at] = part[top // 2:top]
        folded = folded + dot_t(spread(2 * k, count), part[top:, :tail])
        folded = folded + dot_t(spread(2 * k + 1, count), part[top:, tail:])
    folded = folded.astype(bf16)
    mine_ref[:, features:] = folded[:top // 2]
    theirs_ref[:, features:] = folded[top // 2:]


def experts(groups, gate_weight, up_weight, down_weight):
    features, units = gate_weight.shape
    top = 2 * sum(TAKEN)
    rows = top + top // SUB
    wide = groups[0].shape[1]
    return pl.pallas_call(
        functools.partial(expert_kernel, len(groups)),
        out_shape=[jax.ShapeDtypeStruct((top // 2, wide), bf16)] * 2,
        in_specs=[VMEM] * (len(groups) + 3),
        out_specs=[VMEM] * 2,
        scratch_shapes=[
            pltpu.VMEM((rows, features), bf16),
            pltpu.VMEM((top, features // SUB), bf16),
            pltpu.VMEM((rows, 2 * units), f32),
        ],
        compiler_params=pltpu.CompilerParams(vmem_limit_bytes=14 * MIB),
        cost_estimate=pl.CostEstimate(
            flops=6 * rows * features * units, bytes_accessed=6 * features * units, transcendentals=0
        ),
        name="experts",
    )(*groups, gate_weight, up_weight, down_weight)


def add_kernel(a_ref, b_ref, *outs):
    for m, out in enumerate(outs):
        start = PLACED.index(m) * SUB
        rows = slice(start, start + SUB)
        out[...] = (a_ref[rows, :].astype(f32) + b_ref[rows, :].astype(f32)).astype(bf16)


def add(a, b):
    return pl.pallas_call(
        add_kernel,
        out_shape=[jax.ShapeDtypeStruct((SUB, a.shape[1]), bf16)] * EXPERTS,
        in_specs=[VMEM] * 2,
        out_specs=[VMEM] * EXPERTS,
        compiler_params=pltpu.CompilerParams(vmem_limit_bytes=6 * MIB),
        name="add",
    )(a, b)


def combine_kernel(chip_ref, ids_ref, scores_ref, *refs):
    *ins, out_ref, rows_ref = refs
    features = out_ref.shape[1]
    tail = features // SUB
    hit, slot, first, q = routing(ids_ref[...], chip_ref[0])
    scores = scores_ref[...]
    weight = route_factor * scores / (scores[0:1, :] + scores[1:2, :])
    weight = jnp.where(first, weight[0:1, :], weight[1:2, :])
    for m, ref in zip(BACK, ins):
        rows_ref[m * SUB:(m + 1) * SUB, :] = ref[...]

    def weighted(mask, values):
        w = jnp.where(mask, weight, jnp.zeros_like(weight))
        high = w.astype(bf16)
        low = (w - high.astype(f32)).astype(bf16)
        return dot_t(high, values) + dot_t(low, values)

    folded = rows_ref[:, features:]
    for i in range(SUB):
        at = slice(i * tail, (i + 1) * tail)
        total = weighted(hit & (slot == q), rows_ref[:, at])
        total = total + weighted(hit & (slot == SUB) & (q == i), folded)
        out_ref[:, at] = total.astype(bf16)


def combine(chip, ids, scores, buffers, features):
    return pl.pallas_call(
        combine_kernel,
        out_shape=jax.ShapeDtypeStruct((ids.shape[1], features), bf16),
        in_specs=[pl.BlockSpec(memory_space=pltpu.SMEM)] + [VMEM] * (2 + len(buffers)),
        out_specs=VMEM,
        scratch_shapes=[pltpu.VMEM((EXPERTS * SUB, features + features // SUB), bf16)],
        compiler_params=pltpu.CompilerParams(vmem_limit_bytes=12 * MIB),
        name="combine",
    )(chip, ids, scores, *buffers)


def after(values, *others):
    return lax.optimization_barrier((values, others))[0]


def moe_by_chips(moe_input, expert_ids, route_scores, gate_weight, up_weight, down_weight, attention):
    features = moe_input.shape[1]
    members = lax.axis_size("attn")
    chip = (lax.axis_index("attn") // 2).astype(jnp.int32).reshape(1)
    ids, scores = expert_ids.T, route_scores.T
    raw_scores, soften, finish = attention

    def sibling(value):
        return lax.ppermute(value, "attn", [(i, i ^ 1) for i in range(members)])

    def across(value, m):
        return lax.ppermute(value, "attn", [(i, i ^ (2 * m)) for i in range(members)])

    own, along_y, along_z, *far = pack(chip, ids, moe_input)
    far = [across(value, m) for value, m in zip(far, FAR)]
    along_y = across(along_y, 1)
    got = [own, along_y, across(stack(along_z, along_y), 2)] + far
    raw = raw_scores(got[1:2])
    weights, _ = lax.optimization_barrier(((gate_weight, up_weight, down_weight), raw))
    *weights, token = load(*weights)
    mine = got[:3] + [after(value, token) for value in got[3:]]
    theirs = [sibling(value) for value in mine]
    mine, theirs = experts(mine + theirs, *[in_vmem(w) for w in weights])
    total = add(mine, sibling(theirs))
    attn_output = finish(soften(after(raw, *total)))
    back = {0: total[0]}
    for m in (7, 6, 5, 1, 2, 4, 3):
        value = after(total[m], back[5 - m], attn_output) if m in (4, 3) else total[m]
        back[m] = across(value, m)
    moe_output = combine(chip, ids, scores, [back[m] for m in BACK], features)
    return moe_output, attn_output


def slot_table(block_ids):
    flat = block_ids.reshape(-1)
    picks = block_ids.shape[1]
    count = flat.shape[0]
    onehot = (flat[:, None] == jnp.arange(EXPERTS, dtype=jnp.int32)[None, :]).astype(jnp.int32)
    earlier = jnp.arange(count)[:, None] > jnp.arange(count)[None, :]
    same = flat[:, None] == flat[None, :]
    slot = jnp.sum((earlier & same).astype(jnp.int32), axis=1)
    place = flat * CAP + slot
    source = jnp.arange(count, dtype=jnp.int32) // picks + 1
    owner = jnp.zeros((EXPERTS * CAP,), jnp.int32).at[place].set(source) - 1
    return (place, owner)


def expert_rows(received, gate_weight, up_weight, down_weight):
    features = received.shape[-1]
    flat_rows = received.reshape(-1, features)
    gate_part = jnp.dot(flat_rows, gate_weight, preferred_element_type=jnp.float32)
    up_part = jnp.dot(flat_rows, up_weight, preferred_element_type=jnp.float32)
    hidden = (jax.nn.silu(gate_part) * up_part).astype(jnp.bfloat16)
    partial_value = jnp.dot(hidden, down_weight, preferred_element_type=jnp.float32)
    return partial_value.astype(jnp.bfloat16).reshape(received.shape)


def moe_by_slots(moe_input, expert_ids, route_scores, gate_weight, up_weight, down_weight, attention):
    members = lax.axis_size("attn")
    shards = members // EXPERTS
    features = moe_input.shape[1]
    place, owner = slot_table(expert_ids)
    picked = moe_input[jnp.maximum(owner, 0)]
    slot_rows = jnp.where((owner >= 0)[:, None], picked, jnp.zeros_like(picked))
    outbound = jnp.broadcast_to(
        slot_rows.reshape(EXPERTS, 1, CAP, features), (EXPERTS, shards, CAP, features)
    )
    outbound = outbound.reshape(members, CAP, features)
    partial_value = expert_rows(
        lax.all_to_all(outbound, "attn", split_axis=0, concat_axis=0, tiled=True),
        gate_weight,
        up_weight,
        down_weight,
    )
    returned = lax.all_to_all(partial_value, "attn", split_axis=0, concat_axis=0, tiled=True)
    grouped = returned.reshape((EXPERTS, shards) + returned.shape[1:]).astype(jnp.float32)
    expert_out = jnp.sum(grouped, axis=1).astype(jnp.bfloat16)
    combine_weight = route_factor * route_scores / jnp.sum(route_scores, axis=1, keepdims=True)
    token_count, picks = expert_ids.shape
    values = expert_out.reshape(EXPERTS * CAP, features)[place].astype(jnp.float32)
    values = values.reshape(token_count, picks, features)
    moe_output = jnp.sum(values * combine_weight[:, :, None], axis=1).astype(jnp.bfloat16)
    raw_scores, soften, finish = attention
    return moe_output, finish(soften(raw_scores()))


def attend(q_latent, q_rope, latent_cache, rope_cache, cache_lengths):
    seq_count, step_count, _ = q_latent.shape
    cache_len = latent_cache.shape[1]
    latent_width = latent_cache.shape[2]
    rope_width = rope_cache.shape[2]
    head_count = q_latent.shape[2] // latent_width

    def raw_scores(before=()):
        query_rot = q_rope.reshape(seq_count, step_count, head_count, rope_width)
        query_lat = after(q_latent, *before)
        query_lat = query_lat.reshape(seq_count, step_count, head_count, latent_width)
        scores = jnp.einsum(
            "bthc,bpc->bthp", query_lat, latent_cache, preferred_element_type=jnp.float32
        )
        return scores + jnp.einsum(
            "bthc,bpc->bthp", query_rot, rope_cache, preferred_element_type=jnp.float32
        )

    def soften(scores):
        scores = scores * score_factor
        position = jnp.arange(cache_len, dtype=jnp.int32)
        limit = cache_lengths[:, None] - step_count + jnp.arange(step_count, dtype=jnp.int32)[None, :]
        allowed = position[None, None, None, :] <= limit[:, :, None, None]
        scores = jnp.where(allowed, scores, -jnp.inf)
        largest = jnp.max(scores, axis=-1, keepdims=True)
        weights = jnp.exp(scores - largest)
        return (weights / jnp.sum(weights, axis=-1, keepdims=True)).astype(jnp.bfloat16)

    def finish(probs):
        attn = jnp.einsum("bthp,bpc->bthc", probs, latent_cache, preferred_element_type=jnp.float32)
        return attn.astype(jnp.bfloat16).reshape(seq_count, step_count, head_count * latent_width)

    return raw_scores, soften, finish


def body(
    moe_input,
    expert_ids,
    route_scores,
    gate_weight,
    up_weight,
    down_weight,
    q_latent,
    q_rope,
    latent_cache,
    rope_cache,
    cache_lengths,
):
    moe = moe_by_chips if lax.axis_size("attn") == 2 * EXPERTS else moe_by_slots
    attention = attend(q_latent, q_rope, latent_cache, rope_cache, cache_lengths)
    return moe(moe_input, expert_ids, route_scores, gate_weight, up_weight, down_weight, attention)


def solution(mesh):
    placed = (
        P(("rep", "attn"), None),
        P(("rep", "attn"), None),
        P(("rep", "attn"), None),
        P(None, "attn"),
        P(None, "attn"),
        P("attn", None),
        P(("rep", "attn"), None, None),
        P(("rep", "attn"), None, None),
        P(("rep", "attn"), None, None),
        P(("rep", "attn"), None, None),
        P(("rep", "attn")),
    )
    return jax.shard_map(
        body,
        mesh=mesh,
        in_specs=placed,
        out_specs=(P(("rep", "attn"), None), P(("rep", "attn"), None, None)),
        check_vma=False,
    )
```

```python
import functools

import jax
import jax.numpy as jnp
from jax import lax
from jax.experimental import pallas as pl
from jax.experimental.pallas import tpu as pltpu
from jax.sharding import PartitionSpec as P

EXPERTS = 8
CAP = 9
SUB = 8
FOLD = SUB // 2
MIB = 1 << 20
BACK = (7, 6, 5, 4, 3, 2, 1, 0)
PLACED = (0, 1, 2, 3, 4, 5, 6, 7)
HBM = pl.BlockSpec(memory_space=pltpu.HBM)
VMEM = pl.BlockSpec(memory_space=pltpu.VMEM)

score_factor = 192.0 ** (-0.5)
route_factor = 2.5

f32 = jnp.float32
bf16 = jnp.bfloat16


def dot(a, b):
    return jnp.dot(a, b, preferred_element_type=f32)


def dot_t(a, b):
    return lax.dot_general(a, b, (((0,), (0,)), ((), ())), preferred_element_type=f32)


def routing(ids, chip):
    rows = ids.shape[1]
    shape = (EXPERTS * SUB, rows)
    at = lax.broadcasted_iota(jnp.int32, shape, 0)
    expert = jnp.bitwise_xor(at // SUB, chip)
    first = ids[0:1, :] == expert
    hit = first | (ids[1:2, :] == expert)
    r = lax.broadcasted_iota(jnp.int32, (rows, rows), 0)
    c = lax.broadcasted_iota(jnp.int32, (rows, rows), 1)
    slot = dot(hit.astype(f32).astype(bf16), (r < c).astype(f32).astype(bf16)).astype(jnp.int32)
    return hit, slot, first, at % SUB


def ones(mask):
    return jnp.where(mask, 1.0, jnp.zeros(mask.shape, f32)).astype(bf16)


def in_hbm(value):
    return pltpu.with_memory_space_constraint(value, pltpu.HBM)


def in_vmem(value):
    return pltpu.with_memory_space_constraint(value, pltpu.VMEM)


def dot_nt(a, b):
    return lax.dot_general(a, b, (((1,), (1,)), ((), ())), preferred_element_type=f32)


def attend_kernel(lengths_ref, q_ref, q_rope_ref, latent_ref, rope_ref, out_ref, lat_ref, rot_ref):
    seqs, steps, _ = q_ref.shape
    width, turned = latent_ref.shape[2], rope_ref.shape[1]
    heads = q_ref.shape[2] // width

    def one(n, carry):
        for h in range(heads):
            rows = slice(h * steps, (h + 1) * steps)
            lat_ref[rows, :] = q_ref[n, :, h * width:(h + 1) * width]
            rot_ref[rows, :] = q_rope_ref[n, :, h * turned:(h + 1) * turned]
        latent = latent_ref[n]
        scores = (dot_nt(lat_ref[...], latent) + dot(rot_ref[...], rope_ref[n])) * score_factor
        row = lax.broadcasted_iota(jnp.int32, scores.shape, 0)
        position = lax.broadcasted_iota(jnp.int32, scores.shape, 1)
        allowed = position <= lengths_ref[n] - steps + row % steps
        scores = jnp.where(allowed, scores, -jnp.inf)
        weights = jnp.exp(scores - jnp.max(scores, axis=1, keepdims=True))
        probs = (weights / jnp.sum(weights, axis=1, keepdims=True)).astype(bf16)
        attn = dot(probs, latent).astype(bf16)
        for h in range(heads):
            out_ref[n, :, h * width:(h + 1) * width] = attn[h * steps:(h + 1) * steps]
        return carry

    lax.fori_loop(0, seqs, one, 0)


def attend_by_sequence(q_latent, q_rope, latent_cache, rope_cache, lengths):
    width, turned = latent_cache.shape[2], rope_cache.shape[2]
    rows = q_latent.shape[2] // width * q_latent.shape[1]
    arrays = q_latent, q_rope, latent_cache, rope_cache.transpose(0, 2, 1)
    return pl.pallas_call(
        attend_kernel,
        out_shape=jax.ShapeDtypeStruct(q_latent.shape, bf16),
        in_specs=[pl.BlockSpec(memory_space=pltpu.SMEM)] + [VMEM] * 4,
        out_specs=VMEM,
        scratch_shapes=[pltpu.VMEM((rows, width), bf16), pltpu.VMEM((rows, turned), bf16)],
        compiler_params=pltpu.CompilerParams(vmem_limit_bytes=14 * MIB),
        cost_estimate=pl.CostEstimate(
            flops=32 * q_latent.size * latent_cache.shape[1],
            bytes_accessed=2 * (2 * q_latent.size + latent_cache.size),
            transcendentals=0,
        ),
        name="attend",
    )(lengths, *[in_hbm(v) for v in arrays])


def load_kernel(*refs):
    token_ref, sems = refs[-2:]
    token_ref[...] = jnp.zeros_like(token_ref)
    count = len(refs) // 2 - 1
    copies = [pltpu.make_async_copy(refs[i], refs[count + i], sems.at[i]) for i in range(count)]
    for copy in copies:
        copy.start()
    for copy in copies:
        copy.wait()


def load(*weights):
    return pl.pallas_call(
        load_kernel,
        out_shape=[pltpu.VMEM(w.shape, w.dtype) for w in weights] + [jax.ShapeDtypeStruct((8, 128), f32)],
        in_specs=[HBM] * len(weights),
        out_specs=[VMEM] * (len(weights) + 1),
        scratch_shapes=[pltpu.SemaphoreType.DMA((len(weights),))],
        compiler_params=pltpu.CompilerParams(vmem_limit_bytes=MIB),
        cost_estimate=pl.CostEstimate(
            flops=0, bytes_accessed=2 * sum(w.size for w in weights), transcendentals=0
        ),
        name="load",
    )(*[in_hbm(w) for w in weights])


def pack_kernel(chip_ref, ids_ref, x_ref, *outs):
    features = x_ref.shape[1]
    tail = features // SUB
    hit, slot, _, q = routing(ids_ref[...], chip_ref[0])
    main = dot(ones(hit & (slot == q)), x_ref[...]).astype(bf16)
    last = jnp.zeros((EXPERTS * SUB, tail), f32)
    for i in range(SUB):
        last = last + dot(ones(hit & (slot == SUB) & (q == i)), x_ref[:, i * tail:(i + 1) * tail])
    last = last.astype(bf16)
    for m, out in enumerate(outs):
        rows = slice(m * SUB, (m + 1) * SUB)
        out[:, :features] = main[rows]
        out[:, features:] = last[rows]


def pack(chip, ids, x):
    features = x.shape[1]
    return pl.pallas_call(
        pack_kernel,
        out_shape=[jax.ShapeDtypeStruct((SUB, features + features // SUB), bf16)] * EXPERTS,
        in_specs=[pl.BlockSpec(memory_space=pltpu.SMEM)] + [VMEM] * 2,
        out_specs=[VMEM] * EXPERTS,
        compiler_params=pltpu.CompilerParams(vmem_limit_bytes=12 * MIB),
        name="pack",
    )(chip, in_hbm(ids), in_hbm(x))


def spread(i, count):
    j = lax.broadcasted_iota(jnp.int32, (count, count * SUB), 0)
    c = lax.broadcasted_iota(jnp.int32, (count, count * SUB), 1)
    return ones(c == j * SUB + i)


def expert_kernel(groups, *refs):
    ins, (gate_ref, up_ref, down_ref) = refs[:groups], refs[groups:groups + 3]
    mine_ref, theirs_ref = refs[groups + 3:groups + 5]
    rows_ref, tail_ref, acc_ref = refs[groups + 5:]
    features, units = gate_ref.shape
    tail = features // SUB
    top = tail_ref.shape[0]
    count = top // SUB
    wide = 2 * tail
    start = 0
    for ref in ins:
        rows = slice(start, start + SUB)
        rows_ref[rows, :] = ref[:, :features]
        tail_ref[rows, :] = ref[:, features:]
        start += SUB
    folded = tail_ref[...]
    for i in range(SUB):
        rows_ref[top:, i * tail:(i + 1) * tail] = dot(spread(i, count), folded).astype(bf16)
    for k in range(FOLD):
        at = slice(k * wide, (k + 1) * wide)
        for n, ref in enumerate((gate_ref, up_ref)):
            columns = slice(n * units, (n + 1) * units)
            product = dot(rows_ref[:, at], ref[at, :])
            acc_ref[:, columns] = product if k == 0 else acc_ref[:, columns] + product
    hidden = (jax.nn.silu(acc_ref[:, :units]) * acc_ref[:, units:]).astype(bf16)
    folded = jnp.zeros((top, tail), f32)
    for k in range(FOLD):
        at = slice(k * wide, (k + 1) * wide)
        part = dot(hidden, down_ref[:, at]).astype(bf16)
        mine_ref[:, at] = part[:top // 2]
        theirs_ref[:, at] = part[top // 2:top]
        folded = folded + dot_t(spread(2 * k, count), part[top:, :tail])
        folded = folded + dot_t(spread(2 * k + 1, count), part[top:, tail:])
    folded = folded.astype(bf16)
    mine_ref[:, features:] = folded[:top // 2]
    theirs_ref[:, features:] = folded[top // 2:]


def experts(groups, gate_weight, up_weight, down_weight):
    features, units = gate_weight.shape
    top = sum(group.shape[0] for group in groups)
    rows = top + top // SUB
    wide = groups[0].shape[1]
    return pl.pallas_call(
        functools.partial(expert_kernel, len(groups)),
        out_shape=[jax.ShapeDtypeStruct((top // 2, wide), bf16)] * 2,
        in_specs=[VMEM] * (len(groups) + 3),
        out_specs=[VMEM] * 2,
        scratch_shapes=[
            pltpu.VMEM((rows, features), bf16),
            pltpu.VMEM((top, features // SUB), bf16),
            pltpu.VMEM((rows, 2 * units), f32),
        ],
        compiler_params=pltpu.CompilerParams(vmem_limit_bytes=14 * MIB),
        cost_estimate=pl.CostEstimate(
            flops=6 * rows * features * units, bytes_accessed=6 * features * units, transcendentals=0
        ),
        name="experts",
    )(*groups, gate_weight, up_weight, down_weight)


def add_kernel(a_ref, b_ref, *outs):
    for m, out in enumerate(outs):
        start = PLACED.index(m) * SUB
        rows = slice(start, start + SUB)
        out[...] = (a_ref[rows, :].astype(f32) + b_ref[rows, :].astype(f32)).astype(bf16)


def add(a, b):
    return pl.pallas_call(
        add_kernel,
        out_shape=[jax.ShapeDtypeStruct((SUB, a.shape[1]), bf16)] * EXPERTS,
        in_specs=[VMEM] * 2,
        out_specs=[VMEM] * EXPERTS,
        compiler_params=pltpu.CompilerParams(vmem_limit_bytes=6 * MIB),
        name="add",
    )(a, b)


def combine_kernel(chip_ref, ids_ref, scores_ref, *refs):
    *ins, out_ref, rows_ref = refs
    features = out_ref.shape[1]
    tail = features // SUB
    hit, slot, first, q = routing(ids_ref[...], chip_ref[0])
    scores = scores_ref[...]
    weight = route_factor * scores / (scores[0:1, :] + scores[1:2, :])
    weight = jnp.where(first, weight[0:1, :], weight[1:2, :])
    for m, ref in zip(BACK, ins):
        rows_ref[m * SUB:(m + 1) * SUB, :] = ref[...]

    def weighted(mask, values):
        w = jnp.where(mask, weight, jnp.zeros_like(weight))
        high = w.astype(bf16)
        low = (w - high.astype(f32)).astype(bf16)
        return dot_t(high, values) + dot_t(low, values)

    folded = rows_ref[:, features:]
    for i in range(SUB):
        at = slice(i * tail, (i + 1) * tail)
        total = weighted(hit & (slot == q), rows_ref[:, at])
        total = total + weighted(hit & (slot == SUB) & (q == i), folded)
        out_ref[:, at] = total.astype(bf16)


def combine(chip, ids, scores, buffers, features):
    return pl.pallas_call(
        combine_kernel,
        out_shape=jax.ShapeDtypeStruct((ids.shape[1], features), bf16),
        in_specs=[pl.BlockSpec(memory_space=pltpu.SMEM)] + [VMEM] * (2 + len(buffers)),
        out_specs=VMEM,
        scratch_shapes=[pltpu.VMEM((EXPERTS * SUB, features + features // SUB), bf16)],
        compiler_params=pltpu.CompilerParams(vmem_limit_bytes=12 * MIB),
        name="combine",
    )(chip, ids, scores, *buffers)


def after(values, *others):
    return lax.optimization_barrier((values, others))[0]


def moe_by_chips(moe_input, expert_ids, route_scores, gate_weight, up_weight, down_weight, attention):
    features = moe_input.shape[1]
    members = lax.axis_size("attn")
    chip = (lax.axis_index("attn") // 2).astype(jnp.int32).reshape(1)
    ids, scores = expert_ids.T, route_scores.T

    def sibling(value):
        return lax.ppermute(value, "attn", [(i, i ^ 1) for i in range(members)])

    def across(value, m):
        return lax.ppermute(value, "attn", [(i, i ^ (2 * m)) for i in range(members)])

    def exchange(sent, *before):
        got = {0: sent[0]}
        for m in (7, 6, 5, 1, 2, 4, 3):
            value = after(sent[m], got[5 - m], *before) if m in (4, 3) else sent[m]
            got[m] = across(value, m)
        return got

    got = exchange(pack(chip, ids, moe_input))
    *weights, token = load(gate_weight, up_weight, down_weight)
    weights = [in_vmem(w) for w in weights]
    got = [after(got[m], token) if m in (3, 4, 5, 6, 7) else got[m] for m in PLACED]
    theirs = [sibling(value) for value in got]
    mine, theirs = experts(got + theirs, *weights)
    total = add(mine, sibling(theirs))
    attn_output = attend_by_sequence(*attention[:4], after(attention[4], *total))
    back = exchange(total, attn_output)
    moe_output = combine(chip, ids, scores, [back[m] for m in BACK], features)
    return moe_output, attn_output


def slot_table(block_ids):
    flat = block_ids.reshape(-1)
    picks = block_ids.shape[1]
    count = flat.shape[0]
    onehot = (flat[:, None] == jnp.arange(EXPERTS, dtype=jnp.int32)[None, :]).astype(jnp.int32)
    earlier = jnp.arange(count)[:, None] > jnp.arange(count)[None, :]
    same = flat[:, None] == flat[None, :]
    slot = jnp.sum((earlier & same).astype(jnp.int32), axis=1)
    place = flat * CAP + slot
    source = jnp.arange(count, dtype=jnp.int32) // picks + 1
    owner = jnp.zeros((EXPERTS * CAP,), jnp.int32).at[place].set(source) - 1
    return (place, owner)


def expert_rows(received, gate_weight, up_weight, down_weight):
    features = received.shape[-1]
    flat_rows = received.reshape(-1, features)
    gate_part = jnp.dot(flat_rows, gate_weight, preferred_element_type=jnp.float32)
    up_part = jnp.dot(flat_rows, up_weight, preferred_element_type=jnp.float32)
    hidden = (jax.nn.silu(gate_part) * up_part).astype(jnp.bfloat16)
    partial_value = jnp.dot(hidden, down_weight, preferred_element_type=jnp.float32)
    return partial_value.astype(jnp.bfloat16).reshape(received.shape)


def moe_by_slots(moe_input, expert_ids, route_scores, gate_weight, up_weight, down_weight, attention):
    members = lax.axis_size("attn")
    shards = members // EXPERTS
    features = moe_input.shape[1]
    place, owner = slot_table(expert_ids)
    picked = moe_input[jnp.maximum(owner, 0)]
    slot_rows = jnp.where((owner >= 0)[:, None], picked, jnp.zeros_like(picked))
    outbound = jnp.broadcast_to(
        slot_rows.reshape(EXPERTS, 1, CAP, features), (EXPERTS, shards, CAP, features)
    )
    outbound = outbound.reshape(members, CAP, features)
    partial_value = expert_rows(
        lax.all_to_all(outbound, "attn", split_axis=0, concat_axis=0, tiled=True),
        gate_weight,
        up_weight,
        down_weight,
    )
    returned = lax.all_to_all(partial_value, "attn", split_axis=0, concat_axis=0, tiled=True)
    grouped = returned.reshape((EXPERTS, shards) + returned.shape[1:]).astype(jnp.float32)
    expert_out = jnp.sum(grouped, axis=1).astype(jnp.bfloat16)
    combine_weight = route_factor * route_scores / jnp.sum(route_scores, axis=1, keepdims=True)
    token_count, picks = expert_ids.shape
    values = expert_out.reshape(EXPERTS * CAP, features)[place].astype(jnp.float32)
    values = values.reshape(token_count, picks, features)
    moe_output = jnp.sum(values * combine_weight[:, :, None], axis=1).astype(jnp.bfloat16)
    return moe_output, attend(*attention)


def attend(q_latent, q_rope, latent_cache, rope_cache, cache_lengths):
    seq_count, step_count, _ = q_latent.shape
    cache_len = latent_cache.shape[1]
    latent_width = latent_cache.shape[2]
    rope_width = rope_cache.shape[2]
    head_count = q_latent.shape[2] // latent_width
    query_lat = q_latent.reshape(seq_count, step_count, head_count, latent_width)
    query_rot = q_rope.reshape(seq_count, step_count, head_count, rope_width)
    scores = jnp.einsum(
        "bthc,bpc->bthp", query_lat, latent_cache, preferred_element_type=jnp.float32
    )
    scores = scores + jnp.einsum(
        "bthc,bpc->bthp", query_rot, rope_cache, preferred_element_type=jnp.float32
    )
    scores = scores * score_factor
    position = jnp.arange(cache_len, dtype=jnp.int32)
    limit = cache_lengths[:, None] - step_count + jnp.arange(step_count, dtype=jnp.int32)[None, :]
    allowed = position[None, None, None, :] <= limit[:, :, None, None]
    scores = jnp.where(allowed, scores, -jnp.inf)
    largest = jnp.max(scores, axis=-1, keepdims=True)
    weights = jnp.exp(scores - largest)
    probs = (weights / jnp.sum(weights, axis=-1, keepdims=True)).astype(jnp.bfloat16)
    attn = jnp.einsum("bthp,bpc->bthc", probs, latent_cache, preferred_element_type=jnp.float32)
    return attn.astype(jnp.bfloat16).reshape(seq_count, step_count, head_count * latent_width)


def body(
    moe_input,
    expert_ids,
    route_scores,
    gate_weight,
    up_weight,
    down_weight,
    q_latent,
    q_rope,
    latent_cache,
    rope_cache,
    cache_lengths,
):
    moe = moe_by_chips if lax.axis_size("attn") == 2 * EXPERTS else moe_by_slots
    attention = q_latent, q_rope, latent_cache, rope_cache, cache_lengths
    return moe(moe_input, expert_ids, route_scores, gate_weight, up_weight, down_weight, attention)


def solution(mesh):
    placed = (
        P(("rep", "attn"), None),
        P(("rep", "attn"), None),
        P(("rep", "attn"), None),
        P(None, "attn"),
        P(None, "attn"),
        P("attn", None),
        P(("rep", "attn"), None, None),
        P(("rep", "attn"), None, None),
        P(("rep", "attn"), None, None),
        P(("rep", "attn"), None, None),
        P(("rep", "attn")),
    )
    return jax.shard_map(
        body,
        mesh=mesh,
        in_specs=placed,
        out_specs=(P(("rep", "attn"), None), P(("rep", "attn"), None, None)),
        check_vma=False,
    )
```

```python
import functools

import jax
import jax.numpy as jnp
from jax import lax
from jax.experimental import pallas as pl
from jax.experimental.pallas import tpu as pltpu
from jax.sharding import PartitionSpec as P

EXPERTS = 8
CAP = 9
SUB = 8
FOLD = SUB // 2
MIB = 1 << 20
ORDER = (7, 6, 5, 1, 2, 4, 3)
GROUPED = (7, 6, 5, 4, 0, 1, 2, 3)
BACK = (7, 6, 5, 4, 3, 2, 1, 0)
HBM = pl.BlockSpec(memory_space=pltpu.HBM)
VMEM = pl.BlockSpec(memory_space=pltpu.VMEM)

score_factor = 192.0 ** (-0.5)
route_factor = 2.5

f32 = jnp.float32
bf16 = jnp.bfloat16


def dot(a, b):
    return jnp.dot(a, b, preferred_element_type=f32)


def dot_t(a, b):
    return lax.dot_general(a, b, (((0,), (0,)), ((), ())), preferred_element_type=f32)


def routing(ids, chip):
    rows = ids.shape[1]
    shape = (EXPERTS * SUB, rows)
    at = lax.broadcasted_iota(jnp.int32, shape, 0)
    expert = jnp.bitwise_xor(at // SUB, chip)
    first = ids[0:1, :] == expert
    hit = first | (ids[1:2, :] == expert)
    r = lax.broadcasted_iota(jnp.int32, (rows, rows), 0)
    c = lax.broadcasted_iota(jnp.int32, (rows, rows), 1)
    slot = dot(hit.astype(f32).astype(bf16), (r < c).astype(f32).astype(bf16)).astype(jnp.int32)
    return hit, slot, first, at % SUB


def ones(mask):
    return jnp.where(mask, 1.0, jnp.zeros(mask.shape, f32)).astype(bf16)


def in_hbm(value):
    return pltpu.with_memory_space_constraint(value, pltpu.HBM)


def dot_nt(a, b):
    return lax.dot_general(a, b, (((1,), (1,)), ((), ())), preferred_element_type=f32)


def attend_kernel(lengths_ref, q_ref, q_rope_ref, latent_ref, rope_ref, out_ref, lat_ref, rot_ref):
    seqs, steps, _ = q_ref.shape
    width, turned = latent_ref.shape[2], rope_ref.shape[1]
    heads = q_ref.shape[2] // width

    def one(n, carry):
        for h in range(heads):
            rows = slice(h * steps, (h + 1) * steps)
            lat_ref[rows, :] = q_ref[n, :, h * width:(h + 1) * width]
            rot_ref[rows, :] = q_rope_ref[n, :, h * turned:(h + 1) * turned]
        latent = latent_ref[n]
        scores = (dot_nt(lat_ref[...], latent) + dot(rot_ref[...], rope_ref[n])) * score_factor
        row = lax.broadcasted_iota(jnp.int32, scores.shape, 0)
        position = lax.broadcasted_iota(jnp.int32, scores.shape, 1)
        allowed = position <= lengths_ref[n] - steps + row % steps
        scores = jnp.where(allowed, scores, -jnp.inf)
        weights = jnp.exp(scores - jnp.max(scores, axis=1, keepdims=True))
        probs = (weights / jnp.sum(weights, axis=1, keepdims=True)).astype(bf16)
        attn = dot(probs, latent).astype(bf16)
        for h in range(heads):
            out_ref[n, :, h * width:(h + 1) * width] = attn[h * steps:(h + 1) * steps]
        return carry

    lax.fori_loop(0, seqs, one, 0)


def attend_by_sequence(q_latent, q_rope, latent_cache, rope_cache, lengths):
    width, turned = latent_cache.shape[2], rope_cache.shape[2]
    rows = q_latent.shape[2] // width * q_latent.shape[1]
    arrays = q_latent, q_rope, latent_cache, rope_cache.transpose(0, 2, 1)
    return pl.pallas_call(
        attend_kernel,
        out_shape=jax.ShapeDtypeStruct(q_latent.shape, bf16),
        in_specs=[pl.BlockSpec(memory_space=pltpu.SMEM)] + [VMEM] * 4,
        out_specs=VMEM,
        scratch_shapes=[pltpu.VMEM((rows, width), bf16), pltpu.VMEM((rows, turned), bf16)],
        compiler_params=pltpu.CompilerParams(vmem_limit_bytes=14 * MIB),
        cost_estimate=pl.CostEstimate(
            flops=32 * q_latent.size * latent_cache.shape[1],
            bytes_accessed=2 * (2 * q_latent.size + latent_cache.size),
            transcendentals=0,
        ),
        name="attend",
    )(lengths, *[in_hbm(v) for v in arrays])


def pack_kernel(chip_ref, ids_ref, x_ref, *outs):
    features = x_ref.shape[1]
    tail = features // SUB
    hit, slot, _, q = routing(ids_ref[...], chip_ref[0])
    main = dot(ones(hit & (slot == q)), x_ref[...]).astype(bf16)
    last = jnp.zeros((EXPERTS * SUB, tail), f32)
    for i in range(SUB):
        last = last + dot(ones(hit & (slot == SUB) & (q == i)), x_ref[:, i * tail:(i + 1) * tail])
    last = last.astype(bf16)
    for m, out in enumerate(outs):
        out[:, :features] = main[m * SUB:(m + 1) * SUB]
        out[:, features:] = last[m * SUB:(m + 1) * SUB]


def pack(chip, ids, x):
    features = x.shape[1]
    return pl.pallas_call(
        pack_kernel,
        out_shape=[jax.ShapeDtypeStruct((SUB, features + features // SUB), bf16)] * EXPERTS,
        in_specs=[pl.BlockSpec(memory_space=pltpu.SMEM)] + [VMEM] * 2,
        out_specs=[VMEM] * EXPERTS,
        compiler_params=pltpu.CompilerParams(vmem_limit_bytes=12 * MIB),
        name="pack",
    )(chip, in_hbm(ids), in_hbm(x))


def spread(i, count):
    j = lax.broadcasted_iota(jnp.int32, (count, count * SUB), 0)
    c = lax.broadcasted_iota(jnp.int32, (count, count * SUB), 1)
    return ones(c == j * SUB + i)


def expert_kernel(groups, *refs):
    ins, (gate_hbm, up_hbm, down_hbm) = refs[:groups], refs[groups:groups + 3]
    mine_ref, theirs_ref = refs[groups + 3:groups + 5]
    gate_ref, up_ref, down_ref, rows_ref, tail_ref, acc_ref, sems = refs[groups + 5:]
    features, units = gate_ref.shape
    tail = features // SUB
    top = tail_ref.shape[0]
    count = top // SUB
    wide = 2 * tail
    copies = []
    for k in range(FOLD):
        rows = pl.ds(k * wide, wide)
        for ref, to in ((gate_hbm, gate_ref), (up_hbm, up_ref)):
            copies.append(pltpu.make_async_copy(ref.at[rows], to.at[rows], sems.at[len(copies)]))
    for k in range(FOLD):
        columns = pl.ds(k * wide, wide)
        copies.append(pltpu.make_async_copy(down_hbm.at[:, columns], down_ref.at[:, columns], sems.at[len(copies)]))
    for copy in copies:
        copy.start()
    start = 0
    for ref in ins:
        rows = slice(start, start + ref.shape[0])
        rows_ref[rows, :] = ref[:, :features]
        tail_ref[rows, :] = ref[:, features:]
        start += ref.shape[0]
    folded = tail_ref[...]
    for i in range(SUB):
        rows_ref[top:, i * tail:(i + 1) * tail] = dot(spread(i, count), folded).astype(bf16)
    for k in range(FOLD):
        at = slice(k * wide, (k + 1) * wide)
        for n, ref in enumerate((gate_ref, up_ref)):
            copies[2 * k + n].wait()
            columns = slice(n * units, (n + 1) * units)
            product = dot(rows_ref[:, at], ref[at, :])
            acc_ref[:, columns] = product if k == 0 else acc_ref[:, columns] + product
    hidden = (jax.nn.silu(acc_ref[:, :units]) * acc_ref[:, units:]).astype(bf16)
    folded = jnp.zeros((top, tail), f32)
    for k in range(FOLD):
        copies[2 * FOLD + k].wait()
        at = slice(k * wide, (k + 1) * wide)
        part = dot(hidden, down_ref[:, at]).astype(bf16)
        mine_ref[:, at] = part[:top // 2]
        theirs_ref[:, at] = part[top // 2:top]
        folded = folded + dot_t(spread(2 * k, count), part[top:, :tail])
        folded = folded + dot_t(spread(2 * k + 1, count), part[top:, tail:])
    folded = folded.astype(bf16)
    mine_ref[:, features:] = folded[:top // 2]
    theirs_ref[:, features:] = folded[top // 2:]


def experts(groups, gate_weight, up_weight, down_weight):
    features, units = gate_weight.shape
    top = sum(group.shape[0] for group in groups)
    rows = top + top // SUB
    wide = groups[0].shape[1]
    return pl.pallas_call(
        functools.partial(expert_kernel, len(groups)),
        out_shape=[jax.ShapeDtypeStruct((top // 2, wide), bf16)] * 2,
        in_specs=[VMEM] * len(groups) + [HBM] * 3,
        out_specs=[VMEM] * 2,
        scratch_shapes=[
            pltpu.VMEM(gate_weight.shape, bf16),
            pltpu.VMEM(up_weight.shape, bf16),
            pltpu.VMEM(down_weight.shape, bf16),
            pltpu.VMEM((rows, features), bf16),
            pltpu.VMEM((top, features // SUB), bf16),
            pltpu.VMEM((rows, 2 * units), f32),
            pltpu.SemaphoreType.DMA((3 * FOLD,)),
        ],
        compiler_params=pltpu.CompilerParams(vmem_limit_bytes=36 * MIB),
        cost_estimate=pl.CostEstimate(
            flops=6 * rows * features * units, bytes_accessed=6 * features * units, transcendentals=0
        ),
        name="experts",
    )(*groups, gate_weight, up_weight, down_weight)


def add_kernel(a_ref, b_ref, *outs):
    for m, out in enumerate(outs):
        rows = slice(m * SUB, (m + 1) * SUB)
        out[...] = (a_ref[rows, :].astype(f32) + b_ref[rows, :].astype(f32)).astype(bf16)


def add(a, b):
    return pl.pallas_call(
        add_kernel,
        out_shape=[jax.ShapeDtypeStruct((SUB, a.shape[1]), bf16)] * EXPERTS,
        in_specs=[VMEM] * 2,
        out_specs=[VMEM] * EXPERTS,
        compiler_params=pltpu.CompilerParams(vmem_limit_bytes=6 * MIB),
        name="add",
    )(a, b)


def combine_kernel(chip_ref, ids_ref, scores_ref, *refs):
    ins, out_ref, rows_ref = refs[:EXPERTS], refs[EXPERTS], refs[EXPERTS + 1]
    features = out_ref.shape[1]
    tail = features // SUB
    hit, slot, first, q = routing(ids_ref[...], chip_ref[0])
    scores = scores_ref[...]
    weight = route_factor * scores / (scores[0:1, :] + scores[1:2, :])
    weight = jnp.where(first, weight[0:1, :], weight[1:2, :])
    for m, ref in zip(BACK, ins):
        rows_ref[m * SUB:(m + 1) * SUB, :] = ref[...]

    def weighted(mask, values):
        w = jnp.where(mask, weight, jnp.zeros_like(weight))
        high = w.astype(bf16)
        low = (w - high.astype(f32)).astype(bf16)
        return dot_t(high, values) + dot_t(low, values)

    folded = rows_ref[:, features:]
    for i in range(SUB):
        at = slice(i * tail, (i + 1) * tail)
        total = weighted(hit & (slot == q), rows_ref[:, at])
        total = total + weighted(hit & (slot == SUB) & (q == i), folded)
        out_ref[:, at] = total.astype(bf16)


def combine(chip, ids, scores, buffers, features):
    return pl.pallas_call(
        combine_kernel,
        out_shape=jax.ShapeDtypeStruct((ids.shape[1], features), bf16),
        in_specs=[pl.BlockSpec(memory_space=pltpu.SMEM)] + [VMEM] * (2 + EXPERTS),
        out_specs=VMEM,
        scratch_shapes=[pltpu.VMEM((EXPERTS * SUB, features + features // SUB), bf16)],
        compiler_params=pltpu.CompilerParams(vmem_limit_bytes=12 * MIB),
        name="combine",
    )(chip, ids, scores, *buffers)


def after(values, *others):
    return lax.optimization_barrier((values, others))[0]


def moe_by_chips(moe_input, expert_ids, route_scores, gate_weight, up_weight, down_weight, attention):
    features = moe_input.shape[1]
    members = lax.axis_size("attn")
    chip = (lax.axis_index("attn") // 2).astype(jnp.int32).reshape(1)
    ids, scores = expert_ids.T, route_scores.T
    weights = [in_hbm(w) for w in (gate_weight, up_weight, down_weight)]

    def sibling(value):
        return lax.ppermute(value, "attn", [(i, i ^ 1) for i in range(members)])

    def exchange(sent, *first):
        got = {0: sent[0]}
        for m in ORDER:
            value = after(sent[m], got[5 - m], *first) if m in (4, 3) else sent[m]
            got[m] = lax.ppermute(value, "attn", [(i, i ^ (2 * m)) for i in range(members)])
        return got

    got = exchange(pack(chip, ids, moe_input))
    order = GROUPED
    first = jnp.concatenate([got[m] for m in order[:FOLD]], axis=0)
    second = jnp.concatenate([got[m] for m in order[FOLD:]], axis=0)
    mine, theirs = experts([first, second, sibling(first), sibling(second)], *weights)
    total = add(mine, sibling(theirs))
    attn_output = attend_by_sequence(*attention[:4], after(attention[4], *total))
    back = exchange({m: total[place] for place, m in enumerate(order)}, attn_output)
    moe_output = combine(chip, ids, scores, [back[m] for m in BACK], features)
    return moe_output, attn_output


def slot_table(block_ids):
    flat = block_ids.reshape(-1)
    picks = block_ids.shape[1]
    count = flat.shape[0]
    onehot = (flat[:, None] == jnp.arange(EXPERTS, dtype=jnp.int32)[None, :]).astype(jnp.int32)
    earlier = jnp.arange(count)[:, None] > jnp.arange(count)[None, :]
    same = flat[:, None] == flat[None, :]
    slot = jnp.sum((earlier & same).astype(jnp.int32), axis=1)
    place = flat * CAP + slot
    source = jnp.arange(count, dtype=jnp.int32) // picks + 1
    owner = jnp.zeros((EXPERTS * CAP,), jnp.int32).at[place].set(source) - 1
    return (place, owner)


def expert_rows(received, gate_weight, up_weight, down_weight):
    features = received.shape[-1]
    flat_rows = received.reshape(-1, features)
    gate_part = jnp.dot(flat_rows, gate_weight, preferred_element_type=jnp.float32)
    up_part = jnp.dot(flat_rows, up_weight, preferred_element_type=jnp.float32)
    hidden = (jax.nn.silu(gate_part) * up_part).astype(jnp.bfloat16)
    partial_value = jnp.dot(hidden, down_weight, preferred_element_type=jnp.float32)
    return partial_value.astype(jnp.bfloat16).reshape(received.shape)


def moe_by_slots(moe_input, expert_ids, route_scores, gate_weight, up_weight, down_weight, attention):
    members = lax.axis_size("attn")
    shards = members // EXPERTS
    features = moe_input.shape[1]
    place, owner = slot_table(expert_ids)
    picked = moe_input[jnp.maximum(owner, 0)]
    slot_rows = jnp.where((owner >= 0)[:, None], picked, jnp.zeros_like(picked))
    outbound = jnp.broadcast_to(
        slot_rows.reshape(EXPERTS, 1, CAP, features), (EXPERTS, shards, CAP, features)
    )
    outbound = outbound.reshape(members, CAP, features)
    partial_value = expert_rows(
        lax.all_to_all(outbound, "attn", split_axis=0, concat_axis=0, tiled=True),
        gate_weight,
        up_weight,
        down_weight,
    )
    returned = lax.all_to_all(partial_value, "attn", split_axis=0, concat_axis=0, tiled=True)
    grouped = returned.reshape((EXPERTS, shards) + returned.shape[1:]).astype(jnp.float32)
    expert_out = jnp.sum(grouped, axis=1).astype(jnp.bfloat16)
    combine_weight = route_factor * route_scores / jnp.sum(route_scores, axis=1, keepdims=True)
    token_count, picks = expert_ids.shape
    values = expert_out.reshape(EXPERTS * CAP, features)[place].astype(jnp.float32)
    values = values.reshape(token_count, picks, features)
    moe_output = jnp.sum(values * combine_weight[:, :, None], axis=1).astype(jnp.bfloat16)
    return moe_output, attend(*attention)


def attend(q_latent, q_rope, latent_cache, rope_cache, cache_lengths):
    seq_count, step_count, _ = q_latent.shape
    cache_len = latent_cache.shape[1]
    latent_width = latent_cache.shape[2]
    rope_width = rope_cache.shape[2]
    head_count = q_latent.shape[2] // latent_width
    query_lat = q_latent.reshape(seq_count, step_count, head_count, latent_width)
    query_rot = q_rope.reshape(seq_count, step_count, head_count, rope_width)
    scores = jnp.einsum(
        "bthc,bpc->bthp", query_lat, latent_cache, preferred_element_type=jnp.float32
    )
    scores = scores + jnp.einsum(
        "bthc,bpc->bthp", query_rot, rope_cache, preferred_element_type=jnp.float32
    )
    scores = scores * score_factor
    position = jnp.arange(cache_len, dtype=jnp.int32)
    limit = cache_lengths[:, None] - step_count + jnp.arange(step_count, dtype=jnp.int32)[None, :]
    allowed = position[None, None, None, :] <= limit[:, :, None, None]
    scores = jnp.where(allowed, scores, -jnp.inf)
    largest = jnp.max(scores, axis=-1, keepdims=True)
    weights = jnp.exp(scores - largest)
    probs = (weights / jnp.sum(weights, axis=-1, keepdims=True)).astype(jnp.bfloat16)
    attn = jnp.einsum("bthp,bpc->bthc", probs, latent_cache, preferred_element_type=jnp.float32)
    return attn.astype(jnp.bfloat16).reshape(seq_count, step_count, head_count * latent_width)


def body(
    moe_input,
    expert_ids,
    route_scores,
    gate_weight,
    up_weight,
    down_weight,
    q_latent,
    q_rope,
    latent_cache,
    rope_cache,
    cache_lengths,
):
    moe = moe_by_chips if lax.axis_size("attn") == 2 * EXPERTS else moe_by_slots
    attention = q_latent, q_rope, latent_cache, rope_cache, cache_lengths
    return moe(moe_input, expert_ids, route_scores, gate_weight, up_weight, down_weight, attention)


def solution(mesh):
    placed = (
        P(("rep", "attn"), None),
        P(("rep", "attn"), None),
        P(("rep", "attn"), None),
        P(None, "attn"),
        P(None, "attn"),
        P("attn", None),
        P(("rep", "attn"), None, None),
        P(("rep", "attn"), None, None),
        P(("rep", "attn"), None, None),
        P(("rep", "attn"), None, None),
        P(("rep", "attn")),
    )
    return jax.shard_map(
        body,
        mesh=mesh,
        in_specs=placed,
        out_specs=(P(("rep", "attn"), None), P(("rep", "attn"), None, None)),
        check_vma=False,
    )
```

```python
import functools

import jax
import jax.numpy as jnp
from jax import lax
from jax.experimental import pallas as pl
from jax.experimental.pallas import tpu as pltpu
from jax.sharding import PartitionSpec as P

EXPERTS = 8
CAP = 9
SUB = 8
FOLD = SUB // 2
MIB = 1 << 20
ORDER = (7, 6, 5, 1, 2, 4, 3)
GROUPED = (7, 6, 5, 4, 0, 1, 2, 3)
BACK = (7, 6, 5, 4, 3, 2, 1, 0)
HBM = pl.BlockSpec(memory_space=pltpu.HBM)
VMEM = pl.BlockSpec(memory_space=pltpu.VMEM)

score_factor = 192.0 ** (-0.5)
route_factor = 2.5

f32 = jnp.float32
bf16 = jnp.bfloat16


def dot(a, b):
    return jnp.dot(a, b, preferred_element_type=f32)


def dot_t(a, b):
    return lax.dot_general(a, b, (((0,), (0,)), ((), ())), preferred_element_type=f32)


def routing(ids, chip):
    rows = ids.shape[1]
    shape = (EXPERTS * SUB, rows)
    at = lax.broadcasted_iota(jnp.int32, shape, 0)
    expert = jnp.bitwise_xor(at // SUB, chip)
    first = ids[0:1, :] == expert
    hit = first | (ids[1:2, :] == expert)
    r = lax.broadcasted_iota(jnp.int32, (rows, rows), 0)
    c = lax.broadcasted_iota(jnp.int32, (rows, rows), 1)
    slot = dot(hit.astype(f32).astype(bf16), (r < c).astype(f32).astype(bf16)).astype(jnp.int32)
    return hit, slot, first, at % SUB


def ones(mask):
    return jnp.where(mask, 1.0, jnp.zeros(mask.shape, f32)).astype(bf16)


def in_hbm(value):
    return pltpu.with_memory_space_constraint(value, pltpu.HBM)


def dot_nt(a, b):
    return lax.dot_general(a, b, (((1,), (1,)), ((), ())), preferred_element_type=f32)


def attend_kernel(lengths_ref, q_ref, q_rope_ref, latent_ref, rope_ref, out_ref, lat_ref, rot_ref):
    seqs, steps, _ = q_ref.shape
    width, turned = latent_ref.shape[2], rope_ref.shape[1]
    heads = q_ref.shape[2] // width

    def one(n, carry):
        for h in range(heads):
            rows = slice(h * steps, (h + 1) * steps)
            lat_ref[rows, :] = q_ref[n, :, h * width:(h + 1) * width]
            rot_ref[rows, :] = q_rope_ref[n, :, h * turned:(h + 1) * turned]
        latent = latent_ref[n]
        scores = (dot_nt(lat_ref[...], latent) + dot(rot_ref[...], rope_ref[n])) * score_factor
        row = lax.broadcasted_iota(jnp.int32, scores.shape, 0)
        position = lax.broadcasted_iota(jnp.int32, scores.shape, 1)
        allowed = position <= lengths_ref[n] - steps + row % steps
        scores = jnp.where(allowed, scores, -jnp.inf)
        weights = jnp.exp(scores - jnp.max(scores, axis=1, keepdims=True))
        probs = (weights / jnp.sum(weights, axis=1, keepdims=True)).astype(bf16)
        attn = dot(probs, latent).astype(bf16)
        for h in range(heads):
            out_ref[n, :, h * width:(h + 1) * width] = attn[h * steps:(h + 1) * steps]
        return carry

    lax.fori_loop(0, seqs, one, 0)


def attend_by_sequence(q_latent, q_rope, latent_cache, rope_cache, lengths):
    width, turned = latent_cache.shape[2], rope_cache.shape[2]
    rows = q_latent.shape[2] // width * q_latent.shape[1]
    arrays = q_latent, q_rope, latent_cache, rope_cache.transpose(0, 2, 1)
    return pl.pallas_call(
        attend_kernel,
        out_shape=jax.ShapeDtypeStruct(q_latent.shape, bf16),
        in_specs=[pl.BlockSpec(memory_space=pltpu.SMEM)] + [VMEM] * 4,
        out_specs=VMEM,
        scratch_shapes=[pltpu.VMEM((rows, width), bf16), pltpu.VMEM((rows, turned), bf16)],
        compiler_params=pltpu.CompilerParams(vmem_limit_bytes=14 * MIB),
        cost_estimate=pl.CostEstimate(
            flops=32 * q_latent.size * latent_cache.shape[1],
            bytes_accessed=2 * (2 * q_latent.size + latent_cache.size),
            transcendentals=0,
        ),
        name="attend",
    )(lengths, *[in_hbm(v) for v in arrays])


def pack_kernel(chip_ref, ids_ref, x_ref, *outs):
    features = x_ref.shape[1]
    tail = features // SUB
    hit, slot, _, q = routing(ids_ref[...], chip_ref[0])
    main = dot(ones(hit & (slot == q)), x_ref[...]).astype(bf16)
    last = jnp.zeros((EXPERTS * SUB, tail), f32)
    for i in range(SUB):
        last = last + dot(ones(hit & (slot == SUB) & (q == i)), x_ref[:, i * tail:(i + 1) * tail])
    last = last.astype(bf16)
    for m, out in enumerate(outs):
        out[:, :features] = main[m * SUB:(m + 1) * SUB]
        out[:, features:] = last[m * SUB:(m + 1) * SUB]


def pack(chip, ids, x):
    features = x.shape[1]
    return pl.pallas_call(
        pack_kernel,
        out_shape=[jax.ShapeDtypeStruct((SUB, features + features // SUB), bf16)] * EXPERTS,
        in_specs=[pl.BlockSpec(memory_space=pltpu.SMEM)] + [VMEM] * 2,
        out_specs=[VMEM] * EXPERTS,
        compiler_params=pltpu.CompilerParams(vmem_limit_bytes=12 * MIB),
        name="pack",
    )(chip, in_hbm(ids), in_hbm(x))


def spread(i, count):
    j = lax.broadcasted_iota(jnp.int32, (count, count * SUB), 0)
    c = lax.broadcasted_iota(jnp.int32, (count, count * SUB), 1)
    return ones(c == j * SUB + i)


def expert_kernel(groups, *refs):
    ins, (gate_hbm, up_hbm, down_hbm) = refs[:groups], refs[groups:groups + 3]
    mine_ref, theirs_ref = refs[groups + 3:groups + 5]
    gate_ref, up_ref, down_ref, rows_ref, tail_ref, acc_ref, sems = refs[groups + 5:]
    features, units = gate_ref.shape
    tail = features // SUB
    top = tail_ref.shape[0]
    count = top // SUB
    wide = 2 * tail
    copies = []
    for k in range(FOLD):
        rows = pl.ds(k * wide, wide)
        for ref, to in ((gate_hbm, gate_ref), (up_hbm, up_ref)):
            copies.append(pltpu.make_async_copy(ref.at[rows], to.at[rows], sems.at[len(copies)]))
    for k in range(FOLD):
        columns = pl.ds(k * wide, wide)
        copies.append(pltpu.make_async_copy(down_hbm.at[:, columns], down_ref.at[:, columns], sems.at[len(copies)]))
    for copy in copies:
        copy.start()
    start = 0
    for ref in ins:
        rows = slice(start, start + ref.shape[0])
        rows_ref[rows, :] = ref[:, :features]
        tail_ref[rows, :] = ref[:, features:]
        start += ref.shape[0]
    folded = tail_ref[...]
    for i in range(SUB):
        rows_ref[top:, i * tail:(i + 1) * tail] = dot(spread(i, count), folded).astype(bf16)
    for k in range(FOLD):
        at = slice(k * wide, (k + 1) * wide)
        for n, ref in enumerate((gate_ref, up_ref)):
            copies[2 * k + n].wait()
            columns = slice(n * units, (n + 1) * units)
            product = dot(rows_ref[:, at], ref[at, :])
            acc_ref[:, columns] = product if k == 0 else acc_ref[:, columns] + product
    hidden = (jax.nn.silu(acc_ref[:, :units]) * acc_ref[:, units:]).astype(bf16)
    folded = jnp.zeros((top, tail), f32)
    for k in range(FOLD):
        copies[2 * FOLD + k].wait()
        at = slice(k * wide, (k + 1) * wide)
        part = dot(hidden, down_ref[:, at]).astype(bf16)
        mine_ref[:, at] = part[:top // 2]
        theirs_ref[:, at] = part[top // 2:top]
        folded = folded + dot_t(spread(2 * k, count), part[top:, :tail])
        folded = folded + dot_t(spread(2 * k + 1, count), part[top:, tail:])
    folded = folded.astype(bf16)
    mine_ref[:, features:] = folded[:top // 2]
    theirs_ref[:, features:] = folded[top // 2:]


def experts(groups, gate_weight, up_weight, down_weight):
    features, units = gate_weight.shape
    top = sum(group.shape[0] for group in groups)
    rows = top + top // SUB
    wide = groups[0].shape[1]
    return pl.pallas_call(
        functools.partial(expert_kernel, len(groups)),
        out_shape=[jax.ShapeDtypeStruct((top // 2, wide), bf16)] * 2,
        in_specs=[VMEM] * len(groups) + [HBM] * 3,
        out_specs=[VMEM] * 2,
        scratch_shapes=[
            pltpu.VMEM(gate_weight.shape, bf16),
            pltpu.VMEM(up_weight.shape, bf16),
            pltpu.VMEM(down_weight.shape, bf16),
            pltpu.VMEM((rows, features), bf16),
            pltpu.VMEM((top, features // SUB), bf16),
            pltpu.VMEM((rows, 2 * units), f32),
            pltpu.SemaphoreType.DMA((3 * FOLD,)),
        ],
        compiler_params=pltpu.CompilerParams(vmem_limit_bytes=36 * MIB),
        cost_estimate=pl.CostEstimate(
            flops=6 * rows * features * units, bytes_accessed=6 * features * units, transcendentals=0
        ),
        name="experts",
    )(*groups, gate_weight, up_weight, down_weight)


def add_kernel(a_ref, b_ref, *outs):
    for m, out in enumerate(outs):
        rows = slice(m * SUB, (m + 1) * SUB)
        out[...] = (a_ref[rows, :].astype(f32) + b_ref[rows, :].astype(f32)).astype(bf16)


def add(a, b):
    return pl.pallas_call(
        add_kernel,
        out_shape=[jax.ShapeDtypeStruct((SUB, a.shape[1]), bf16)] * EXPERTS,
        in_specs=[VMEM] * 2,
        out_specs=[VMEM] * EXPERTS,
        compiler_params=pltpu.CompilerParams(vmem_limit_bytes=6 * MIB),
        name="add",
    )(a, b)


def combine_kernel(chip_ref, ids_ref, scores_ref, *refs):
    ins, out_ref, rows_ref = refs[:EXPERTS], refs[EXPERTS], refs[EXPERTS + 1]
    features = out_ref.shape[1]
    tail = features // SUB
    hit, slot, first, q = routing(ids_ref[...], chip_ref[0])
    scores = scores_ref[...]
    weight = route_factor * scores / (scores[0:1, :] + scores[1:2, :])
    weight = jnp.where(first, weight[0:1, :], weight[1:2, :])
    for m, ref in zip(BACK, ins):
        rows_ref[m * SUB:(m + 1) * SUB, :] = ref[...]

    def weighted(mask, values):
        w = jnp.where(mask, weight, jnp.zeros_like(weight))
        high = w.astype(bf16)
        low = (w - high.astype(f32)).astype(bf16)
        return dot_t(high, values) + dot_t(low, values)

    folded = rows_ref[:, features:]
    for i in range(SUB):
        at = slice(i * tail, (i + 1) * tail)
        total = weighted(hit & (slot == q), rows_ref[:, at])
        total = total + weighted(hit & (slot == SUB) & (q == i), folded)
        out_ref[:, at] = total.astype(bf16)


def combine(chip, ids, scores, buffers, features):
    return pl.pallas_call(
        combine_kernel,
        out_shape=jax.ShapeDtypeStruct((ids.shape[1], features), bf16),
        in_specs=[pl.BlockSpec(memory_space=pltpu.SMEM)] + [VMEM] * (2 + EXPERTS),
        out_specs=VMEM,
        scratch_shapes=[pltpu.VMEM((EXPERTS * SUB, features + features // SUB), bf16)],
        compiler_params=pltpu.CompilerParams(vmem_limit_bytes=12 * MIB),
        name="combine",
    )(chip, ids, scores, *buffers)


def after(values, *others):
    return lax.optimization_barrier((values, others))[0]


def moe_by_chips(moe_input, expert_ids, route_scores, gate_weight, up_weight, down_weight, attention):
    features = moe_input.shape[1]
    members = lax.axis_size("attn")
    chip = (lax.axis_index("attn") // 2).astype(jnp.int32).reshape(1)
    ids, scores = expert_ids.T, route_scores.T
    weights = [in_hbm(w) for w in (gate_weight, up_weight, down_weight)]

    def sibling(value):
        return lax.ppermute(value, "attn", [(i, i ^ 1) for i in range(members)])

    def exchange(sent, *first):
        got = {0: sent[0]}
        for m in ORDER:
            value = after(sent[m], got[5 - m], *first) if m in (4, 3) else sent[m]
            got[m] = lax.ppermute(value, "attn", [(i, i ^ (2 * m)) for i in range(members)])
        return got

    got = exchange(pack(chip, ids, moe_input))
    order = GROUPED
    first = jnp.concatenate([got[m] for m in order[:FOLD]], axis=0)
    second = jnp.concatenate([got[m] for m in order[FOLD:]], axis=0)
    mine, theirs = experts([first, second, sibling(first), sibling(second)], *weights)
    total = add(mine, sibling(theirs))
    attn_output = attend_by_sequence(*attention[:4], after(attention[4], *total))
    back = exchange({m: total[place] for place, m in enumerate(order)})
    moe_output = combine(chip, ids, scores, [back[m] for m in BACK], features)
    return moe_output, attn_output


def slot_table(block_ids):
    flat = block_ids.reshape(-1)
    picks = block_ids.shape[1]
    count = flat.shape[0]
    onehot = (flat[:, None] == jnp.arange(EXPERTS, dtype=jnp.int32)[None, :]).astype(jnp.int32)
    earlier = jnp.arange(count)[:, None] > jnp.arange(count)[None, :]
    same = flat[:, None] == flat[None, :]
    slot = jnp.sum((earlier & same).astype(jnp.int32), axis=1)
    place = flat * CAP + slot
    source = jnp.arange(count, dtype=jnp.int32) // picks + 1
    owner = jnp.zeros((EXPERTS * CAP,), jnp.int32).at[place].set(source) - 1
    return (place, owner)


def expert_rows(received, gate_weight, up_weight, down_weight):
    features = received.shape[-1]
    flat_rows = received.reshape(-1, features)
    gate_part = jnp.dot(flat_rows, gate_weight, preferred_element_type=jnp.float32)
    up_part = jnp.dot(flat_rows, up_weight, preferred_element_type=jnp.float32)
    hidden = (jax.nn.silu(gate_part) * up_part).astype(jnp.bfloat16)
    partial_value = jnp.dot(hidden, down_weight, preferred_element_type=jnp.float32)
    return partial_value.astype(jnp.bfloat16).reshape(received.shape)


def moe_by_slots(moe_input, expert_ids, route_scores, gate_weight, up_weight, down_weight, attention):
    members = lax.axis_size("attn")
    shards = members // EXPERTS
    features = moe_input.shape[1]
    place, owner = slot_table(expert_ids)
    picked = moe_input[jnp.maximum(owner, 0)]
    slot_rows = jnp.where((owner >= 0)[:, None], picked, jnp.zeros_like(picked))
    outbound = jnp.broadcast_to(
        slot_rows.reshape(EXPERTS, 1, CAP, features), (EXPERTS, shards, CAP, features)
    )
    outbound = outbound.reshape(members, CAP, features)
    partial_value = expert_rows(
        lax.all_to_all(outbound, "attn", split_axis=0, concat_axis=0, tiled=True),
        gate_weight,
        up_weight,
        down_weight,
    )
    returned = lax.all_to_all(partial_value, "attn", split_axis=0, concat_axis=0, tiled=True)
    grouped = returned.reshape((EXPERTS, shards) + returned.shape[1:]).astype(jnp.float32)
    expert_out = jnp.sum(grouped, axis=1).astype(jnp.bfloat16)
    combine_weight = route_factor * route_scores / jnp.sum(route_scores, axis=1, keepdims=True)
    token_count, picks = expert_ids.shape
    values = expert_out.reshape(EXPERTS * CAP, features)[place].astype(jnp.float32)
    values = values.reshape(token_count, picks, features)
    moe_output = jnp.sum(values * combine_weight[:, :, None], axis=1).astype(jnp.bfloat16)
    return moe_output, attend(*attention)


def attend(q_latent, q_rope, latent_cache, rope_cache, cache_lengths):
    seq_count, step_count, _ = q_latent.shape
    cache_len = latent_cache.shape[1]
    latent_width = latent_cache.shape[2]
    rope_width = rope_cache.shape[2]
    head_count = q_latent.shape[2] // latent_width
    query_lat = q_latent.reshape(seq_count, step_count, head_count, latent_width)
    query_rot = q_rope.reshape(seq_count, step_count, head_count, rope_width)
    scores = jnp.einsum(
        "bthc,bpc->bthp", query_lat, latent_cache, preferred_element_type=jnp.float32
    )
    scores = scores + jnp.einsum(
        "bthc,bpc->bthp", query_rot, rope_cache, preferred_element_type=jnp.float32
    )
    scores = scores * score_factor
    position = jnp.arange(cache_len, dtype=jnp.int32)
    limit = cache_lengths[:, None] - step_count + jnp.arange(step_count, dtype=jnp.int32)[None, :]
    allowed = position[None, None, None, :] <= limit[:, :, None, None]
    scores = jnp.where(allowed, scores, -jnp.inf)
    largest = jnp.max(scores, axis=-1, keepdims=True)
    weights = jnp.exp(scores - largest)
    probs = (weights / jnp.sum(weights, axis=-1, keepdims=True)).astype(jnp.bfloat16)
    attn = jnp.einsum("bthp,bpc->bthc", probs, latent_cache, preferred_element_type=jnp.float32)
    return attn.astype(jnp.bfloat16).reshape(seq_count, step_count, head_count * latent_width)


def body(
    moe_input,
    expert_ids,
    route_scores,
    gate_weight,
    up_weight,
    down_weight,
    q_latent,
    q_rope,
    latent_cache,
    rope_cache,
    cache_lengths,
):
    moe = moe_by_chips if lax.axis_size("attn") == 2 * EXPERTS else moe_by_slots
    attention = q_latent, q_rope, latent_cache, rope_cache, cache_lengths
    return moe(moe_input, expert_ids, route_scores, gate_weight, up_weight, down_weight, attention)


def solution(mesh):
    placed = (
        P(("rep", "attn"), None),
        P(("rep", "attn"), None),
        P(("rep", "attn"), None),
        P(None, "attn"),
        P(None, "attn"),
        P("attn", None),
        P(("rep", "attn"), None, None),
        P(("rep", "attn"), None, None),
        P(("rep", "attn"), None, None),
        P(("rep", "attn"), None, None),
        P(("rep", "attn")),
    )
    return jax.shard_map(
        body,
        mesh=mesh,
        in_specs=placed,
        out_specs=(P(("rep", "attn"), None), P(("rep", "attn"), None, None)),
        check_vma=False,
    )
```
